256 devices in a mesh: seq: 32 (over z, y_hi, core), head: 8 (over x, y_lo).
Axes of the slice: x: 4, y: 4 (y_hi: 2, y_lo: 2; y = y_hi * 2 + y_lo), z: 8, core: 2. Of those that a mesh axis runs over, the one named last changes fastest.
Arguments:
- query_raw: bfloat16 [8192, 8192], P('seq', 'head'), may hold values from -208 to 208
- key_raw: bfloat16 [8192, 8192], P('seq', 'head'), may hold values from -208 to 208
- values: bfloat16 [8192, 8192], P('seq', 'head'), may hold values from -6 to 6
- out_grad: bfloat16 [8192, 8192], P('seq', 'head'), may hold values from -6 to 6
- attn_out: bfloat16 [8192, 8192], P('seq', 'head'), may hold values from -4 to 4
- log_norm: float32 [64, 8192], P('head', 'seq'), may hold values from 6 to 10
- query_gain: float32 [8192], P('head'), may hold values from 0.1 to 1.9
- key_gain: float32 [8192], P('head'), may hold values from 0.1 to 1.9
- block_order: int32 [64], replicated, may hold values from 0 to 63, as said below
Outputs:
- query_grad: bfloat16 [8192, 8192], P('seq', 'head')
- key_grad: bfloat16 [8192, 8192], P('seq', 'head')
- value_grad: bfloat16 [8192, 8192], P('seq', 'head')
The draws below stay inside these ranges and needn't reach their ends.
Inputs may be any that keep to these rules, and one draw needn't show every extreme that they name: block_order is a permutation of 0 to 63; stored blocks 2 g and 2 g + 1 of each group g hold positions p and 63 - p, in either order, for some p below 32.
All inputs are finite; a program needn't handle non-finite values.
Results may differ from the reference program's by a relative error of at most 0.012.
Values may be sent and summed in bfloat16 or wider, within the bound.
A program may use at most 64 MiB of HBM per device.

```python
import jax
import jax.numpy as jnp
from jax import lax

HEADS = 64
HD = 128
BLK = 128
WINDOW = 4
GROUPS = 32
NB = 64
TOKENS = 8192
WIDTH = 8192


def scales(key, growth, row_top, flip):
    key_cols, key_rows = jax.random.split(key)
    position = jnp.arange(WIDTH, dtype=jnp.float32) / (WIDTH - 1)
    tilt = jnp.abs(position - flip)
    spread = jnp.exp(jax.random.uniform(key_cols, (WIDTH,), jnp.float32) * jnp.log(10.0))
    row_scale = jnp.exp(jax.random.uniform(key_rows, (TOKENS, 1), jnp.float32) * jnp.log(row_top))
    return row_scale * spread[None, :] * jnp.exp(tilt * jnp.log(growth))[None, :]


def draw_query_raw(key, part):
    key = jax.random.fold_in(key, 11)
    key_scale, key_vals = jax.random.split(key)
    entries = jnp.clip(jax.random.normal(key_vals, (TOKENS, WIDTH), jnp.float32), -4.0, 4.0)
    field = entries * scales(key_scale, 1.7320508, 1.0, 0.0)
    return field.astype(jnp.bfloat16)


def draw_key_raw(key, part):
    key = jax.random.fold_in(key, 12)
    key_scale, key_vals = jax.random.split(key)
    entries = jnp.clip(jax.random.normal(key_vals, (TOKENS, WIDTH), jnp.float32), -4.0, 4.0)
    field = entries * scales(key_scale, 1.7320508, 1.0, 1.0)
    return field.astype(jnp.bfloat16)


def draw_block_order(key, part):
    key = jax.random.fold_in(key, 13)
    key_perm, key_flip = jax.random.split(key)
    lower = jax.random.permutation(key_perm, GROUPS).astype(jnp.int32)
    upper = 2 * GROUPS - 1 - lower
    flipped = jax.random.randint(key_flip, (GROUPS,), 0, 2, dtype=jnp.int32)
    first = jnp.where(flipped == 1, upper, lower)
    second = jnp.where(flipped == 1, lower, upper)
    return jnp.stack([first, second], axis=1).reshape(NB).astype(jnp.int32)


def level_of(own_key, dims, cuts, smallest, largest):
    level = 1.0
    for dim, blocks in cuts:
        heights = jax.random.uniform(jax.random.fold_in(jax.random.fold_in(own_key, 6), dim), (blocks,), jnp.float32, smallest / len(cuts), largest / len(cuts))
        level = level * jnp.repeat(jnp.exp(heights), dims[dim] // blocks).reshape((-1,) + (1,) * (len(dims) - 1 - dim))
    return level


def gaussian(rng, shape, width, reach, cuts=(), kind=jnp.bfloat16):
    values = jax.random.normal(rng, shape, jnp.float32) * width
    if len(cuts) > 0:
        values = level_of(rng, shape, cuts, -0.22, 0.18) * values
    return jnp.clip(values, min=-reach, max=reach).astype(kind)


def setup_inputs(seed: int = 0) -> dict:
    seeds = jax.random.split(jax.random.key(seed), 10)
    query_raw = draw_query_raw(jax.random.fold_in(seeds[9], 71), 0)
    key_raw = draw_key_raw(jax.random.fold_in(seeds[9], 71), 0)
    values = gaussian(seeds[2], (TOKENS, WIDTH), 1.0, 6.0, ((0, 32), (1, 8)))
    out_grad = gaussian(seeds[3], (TOKENS, WIDTH), 1.0, 6.0, ((0, 32), (1, 8)))
    attn_out = gaussian(seeds[4], (TOKENS, WIDTH), 0.3, 4.0, ((0, 32), (1, 8)))
    log_norm = jnp.clip(6.0 + 4.0 * jax.random.uniform(seeds[5], (HEADS, TOKENS), jnp.float32) ** level_of(seeds[5], (HEADS, TOKENS), ((0, 8), (1, 32)), -0.2, 0.2), 6.0, 10.0)
    query_gain = jnp.clip(1.0 + 0.18 * jax.random.normal(seeds[6], (WIDTH,), jnp.float32), 0.1, 1.9)
    key_gain = jnp.clip(1.0 + 0.18 * jax.random.normal(seeds[7], (WIDTH,), jnp.float32), 0.1, 1.9)
    block_order = draw_block_order(jax.random.fold_in(seeds[9], 71), 0)
    return {"query_raw": query_raw, "key_raw": key_raw, "values": values, "out_grad": out_grad, "attn_out": attn_out, "log_norm": log_norm, "query_gain": query_gain, "key_gain": key_gain, "block_order": block_order}


EPSILON = 1e-06

def normalize(raw, gain):
    entries = raw.astype(jnp.float32)
    row_scale = lax.rsqrt(lax.optimization_barrier(jnp.mean(entries * entries, axis=1)) + EPSILON)
    return (entries * row_scale[:, None] * gain[None, :]).astype(jnp.bfloat16)

def rounded(matrix):
    return lax.optimization_barrier(matrix.astype(jnp.bfloat16)).astype(jnp.float32)

def reference(query_raw, key_raw, values, out_grad, attn_out, log_norm, query_gain, key_gain, block_order):
    group_rows = 2 * BLK
    score_scale = HD ** (-0.5)
    query_normed = normalize(query_raw, query_gain)
    key_normed = normalize(key_raw, key_gain)
    slot_order = block_order.astype(jnp.int32).reshape(GROUPS, 2)
    offsets = jnp.arange(BLK, dtype=jnp.int32)
    positions = (slot_order[:, :, None] * BLK + offsets[None, None, :]).reshape(GROUPS, group_rows)

    def one_head(head_idx):
        start = head_idx * HD

        def columns(array):
            piece = lax.dynamic_slice_in_dim(array, start, HD, 1)
            return piece.reshape(GROUPS, group_rows, HD).astype(jnp.float32)
        query_head = columns(query_normed)
        key_head = columns(key_normed)
        value_head = columns(values)
        grad_head = columns(out_grad)
        out_head = columns(attn_out)
        row_delta = lax.optimization_barrier(jnp.sum(grad_head * out_head, axis=2))
        norm_head = lax.dynamic_index_in_dim(log_norm, head_idx, 0, keepdims=False).reshape(GROUPS, group_rows)
        query_acc = jnp.zeros((GROUPS, group_rows, HD), jnp.float32)
        key_acc = jnp.zeros((GROUPS, group_rows, HD), jnp.float32)
        value_acc = jnp.zeros((GROUPS, group_rows, HD), jnp.float32)
        for cycle_step in range(WINDOW):
            keys_at = jnp.roll(key_head, cycle_step, axis=0)
            values_at = jnp.roll(value_head, cycle_step, axis=0)
            key_pos = jnp.roll(positions, cycle_step, axis=0)
            scores = jnp.einsum('aqd,akd->aqk', query_head, keys_at) * score_scale
            visible = key_pos[:, None, :] <= positions[:, :, None]
            probs = jnp.where(visible, jnp.exp(scores - norm_head[:, :, None]), 0.0)
            dprobs = jnp.einsum('aqd,akd->aqk', grad_head, values_at)
            dscores = probs * (dprobs - row_delta[:, :, None])
            probs_low = rounded(probs)
            dscores_low = rounded(dscores)
            query_acc = query_acc + jnp.einsum('aqk,akd->aqd', dscores_low, keys_at) * score_scale
            key_term = jnp.einsum('aqk,aqd->akd', dscores_low, query_head) * score_scale
            value_term = jnp.einsum('aqk,aqd->akd', probs_low, grad_head)
            key_acc = key_acc + jnp.roll(key_term, -cycle_step, axis=0)
            value_acc = value_acc + jnp.roll(value_term, -cycle_step, axis=0)
        stacked = jnp.stack([query_acc, key_acc, value_acc]).reshape(3, GROUPS * group_rows, HD)
        return stacked.astype(jnp.bfloat16)
    grads = lax.map(one_head, jnp.arange(HEADS, dtype=jnp.int32))
    grads = grads.transpose(1, 2, 0, 3).reshape(3, TOKENS, HEADS * HD)
    return (grads[0], grads[1], grads[2])
```

```python
import functools

import jax
import jax.numpy as jnp
from jax import lax
from jax.experimental import pallas as pl
from jax.experimental.pallas import tpu as pltpu
from jax.sharding import PartitionSpec as P

EPSILON = 1e-06
LOG2E = 1.4426950408889634
MESH = pl.DeviceIdType.MESH
F32 = jnp.float32
BF16 = jnp.bfloat16
HALF = 4
BLK = 128
ROWS = 256
HD = 128

NT = (((1,), (1,)), ((), ()))
NN = (((1,), (0,)), ((), ()))


def dot(a, b, dims):
    return lax.dot_general(a, b, dims, preferred_element_type=F32)


def head_cols(head):
    return pl.ds(pl.multiple_of(head * HD, HD), HD)


def kernel(
    seq_count,
    head_count,
    order,
    q_hbm,
    k_hbm,
    v_hbm,
    g_hbm,
    o_hbm,
    norm_ref,
    q_gain,
    k_gain,
    dq_out,
    dk_out,
    dv_out,
    q_all,
    k_all,
    g_all,
    o_all,
    q_own,
    g_own,
    k_own,
    v_own,
    k_flip,
    stats,
    q_stage,
    k_stage,
    stats_stage,
    squares,
    q_next,
    g_next,
    stats_next,
    q_far,
    g_far,
    stats_far,
    dq_acc,
    dk_acc,
    dv_acc,
    next_stage,
    next_back,
    far_stage,
    far_back,
    dq_stage,
    dk_stage,
    dv_stage,
    load_sem,
    load_g_sem,
    load_v_sem,
    sq_sem,
    xg_sem,
    xv_sem,
    xq_sem,
    xk_sem,
    xs_sem,
    ng_sem,
    nq_sem,
    ns_sem,
    fg_sem,
    fq_sem,
    fs_sem,
    nb_sem,
    fb_sem,
    od_sem,
    oq_sem,
    ok_sem,
    ov_sem,
):
    seq = lax.axis_index("seq")
    head = lax.axis_index("head")
    chip = seq // 2
    core = seq % 2
    other = 1 - core
    chips = seq_count // 2
    width = head_count * q_hbm.shape[1]
    score_scale = HD ** (-0.5)

    sibling = (chip * 2 + other, head)
    prev = (((chip + chips - 1) % chips) * 2 + core, head)
    succ = (((chip + 1) % chips) * 2 + core, head)
    prev_far = (((chip + chips - 2) % chips) * 2 + core, head)
    succ_far = (((chip + 2) % chips) * 2 + core, head)

    def remote(src, dst, sem, idx, device):
        return pltpu.make_async_remote_copy(
            src_ref=src,
            dst_ref=dst,
            send_sem=sem.at[(0, *idx)],
            recv_sem=sem.at[(1, *idx)],
            device_id=device,
            device_id_type=MESH,
        )

    loads = [
        pltpu.make_async_copy(src, dst, load_sem.at[n])
        for n, (src, dst) in enumerate(
            ((q_hbm, q_all), (k_hbm, k_all), (g_hbm, g_all), (o_hbm, o_all))
        )
    ]

    def load_g(h):
        return pltpu.make_async_copy(
            g_hbm.at[:, head_cols(core * HALF + h)], g_own.at[h, core], load_g_sem.at[h]
        )

    def load_v(h):
        return pltpu.make_async_copy(
            v_hbm.at[:, head_cols(core * HALF + h)], v_own.at[h, core], load_v_sem.at[h]
        )

    loads[0].start()
    loads[1].start()
    for h in range(HALF):
        load_g(h).start()
    loads[2].start()
    loads[3].start()
    for h in range(HALF):
        load_v(h).start()

    barrier = pltpu.get_barrier_semaphore()
    for device in (sibling, prev, succ, prev_far, succ_far):
        pl.semaphore_signal(barrier, inc=1, device_id=device, device_id_type=MESH)
    for n in range(1, head_count):
        pl.semaphore_signal(
            barrier, inc=1, device_id=(seq, (head + n) % head_count), device_id_type=MESH
        )
    pl.semaphore_wait(barrier, 5 + head_count - 1)

    def give_g(h):
        return remote(
            g_hbm.at[:, head_cols(other * HALF + h)], g_own.at[h, core], xg_sem, (h,), sibling
        )

    def give_v(h):
        return remote(
            v_hbm.at[:, head_cols(other * HALF + h)], v_own.at[h, core], xv_sem, (h,), sibling
        )

    def give_q(h):
        return remote(q_stage.at[h], q_own.at[h, core], xq_sem, (h,), sibling)

    def give_k(h):
        return remote(k_stage.at[h], k_own.at[h, core], xk_sem, (h,), sibling)

    give_s = remote(stats_stage, stats.at[core], xs_sem, (0,), sibling)

    def send_g(h, g):
        return remote(g_own.at[h, g], g_next.at[h, g], ng_sem, (h, g), prev)

    def send_q(h, g):
        return remote(q_own.at[h, g], q_next.at[h, g], nq_sem, (h, g), prev)

    send_s = remote(stats, stats_next, ns_sem, (0,), prev)

    def send_far_g(h):
        return remote(g_own.at[h, 0], g_far.at[h], fg_sem, (h,), prev_far)

    def send_far_q(h):
        return remote(q_own.at[h, 0], q_far.at[h], fq_sem, (h,), prev_far)

    send_far_s = remote(stats.at[0], stats_far, fs_sem, (0,), prev_far)

    def back_next(h, g):
        return remote(next_stage.at[h, g], next_back.at[h, g], nb_sem, (h, g), succ)

    def back_far(h):
        return remote(far_stage.at[h], far_back.at[h], fb_sem, (h,), succ_far)

    def over_heads(body):
        lax.fori_loop(0, HALF, lambda h, c: (body(h), c)[1], 0)

    over_heads(lambda h: give_g(h).start())

    def first_g(h):
        load_g(h).wait()
        send_g(h, core).start()

        @pl.when(core == 0)
        def _():
            send_far_g(h).start()

    over_heads(first_g)

    def row_sums(src):
        def add(h, total):
            block = src[:, head_cols(h)].astype(F32)
            return total + block * block

        total = lax.fori_loop(0, 2 * HALF, add, jnp.zeros((ROWS, HD), F32))
        return jnp.sum(total.T, axis=0, keepdims=True)

    loads[0].wait()
    loads[1].wait()
    squares[0] = jnp.zeros((8, ROWS), F32)
    squares[0, 0:1, :] = row_sums(q_all)
    squares[0, 1:2, :] = row_sums(k_all)
    sq_copies = []
    for n in range(1, head_count):
        copy = remote(
            squares.at[0], squares.at[n], sq_sem, (n,), (seq, (head + n) % head_count)
        )
        copy.start()
        sq_copies.append(copy)

    over_heads(lambda h: give_v(h).start())

    loads[2].wait()
    loads[3].wait()
    norm_rows = norm_ref[...] * LOG2E

    def delta_row(h):
        product = g_all[:, head_cols(h)].astype(F32) * o_all[:, head_cols(h)].astype(F32)
        return jnp.sum(product.T, axis=0, keepdims=True)

    first_half = core == 0
    stats[core, 0:HALF, :] = jnp.where(first_half, norm_rows[0:HALF], norm_rows[HALF:])
    stats_stage[0:HALF, :] = jnp.where(first_half, norm_rows[HALF:], norm_rows[0:HALF])
    for h in range(HALF):
        stats[core, HALF + h : HALF + h + 1, :] = delta_row(core * HALF + h)
        stats_stage[HALF + h : HALF + h + 1, :] = delta_row(other * HALF + h)
    give_s.start()

    def second_g(h):
        give_g(h).wait_recv()
        send_g(h, other).start()

        @pl.when(core == 1)
        def _():
            send_far_g(h).start()

    over_heads(second_g)
    give_s.wait_recv()
    send_s.start()
    send_far_s.start()

    for copy in sq_copies:
        copy.wait_recv()
    total = squares[0, 0:2, :]
    for n in range(1, head_count):
        total = total + squares[n, 0:2, :]
    scale = lax.rsqrt(total / width + EPSILON)
    q_scale = jnp.broadcast_to(scale[0:1, :], (HD, ROWS)).T
    k_scale = jnp.broadcast_to(scale[1:2, :], (HD, ROWS)).T

    def normed(src, scales, gain, h):
        return (src[:, head_cols(h)].astype(F32) * scales * gain[0:1, head_cols(h)]).astype(BF16)

    def norm_q(h):
        q_stage[h] = normed(q_all, q_scale, q_gain, other * HALF + h)
        give_q(h).start()
        q_own[h, core] = normed(q_all, q_scale, q_gain, core * HALF + h)
        send_q(h, core).start()

        @pl.when(core == 0)
        def _():
            send_far_q(h).start()

    over_heads(norm_q)

    def norm_k(h):
        k_stage[h] = normed(k_all, k_scale, k_gain, other * HALF + h)
        give_k(h).start()
        mine = normed(k_all, k_scale, k_gain, core * HALF + h)
        k_own[h, core] = mine
        k_flip[h, core] = mine.T

    over_heads(norm_k)

    def second_q(h):
        give_q(h).wait_recv()
        send_q(h, other).start()

        @pl.when(core == 1)
        def _():
            send_far_q(h).start()

    over_heads(second_q)

    def ready_kv(h):
        give_k(h).wait_recv()
        k_flip[h, other] = k_own[h, other].T
        give_v(h).wait_recv()
        load_v(h).wait()

    over_heads(ready_kv)

    def group_of(step):
        return (chip * 2 + step) % seq_count

    def key_pos(c):
        group = group_of(c)
        row = lax.broadcasted_iota(jnp.int32, (ROWS, ROWS), 0)
        return row + jnp.where(row < BLK, order[2 * group] * BLK, order[2 * group + 1] * BLK - BLK)

    def query_pos(step):
        group = group_of(step)
        col = lax.broadcasted_iota(jnp.int32, (1, ROWS), 1)
        return col + jnp.where(col < BLK, order[2 * group] * BLK, order[2 * group + 1] * BLK - BLK)

    def pair(h, c, q, g, norm_row, delta, q_at):
        s = dot(k_own[h, c], q, NT)
        d = dot(v_own[h, c], g, NT)
        p = jnp.exp2(s * (score_scale * LOG2E) - norm_row)
        p = jnp.where(key_pos(c) <= q_at, p, 0.0)
        ds = (p * (d - delta)).astype(BF16)
        dv_add = dot(p.astype(BF16), g, NN)
        dk_add = dot(ds, q, NN)
        dq_add = dot(k_flip[h, c], ds, NN)
        return dq_add, dk_add, dv_add

    def out_copy(stage, out, sem, n, h):
        mine = pltpu.make_async_copy(
            stage.at[h, core], out.at[:, head_cols(core * HALF + h)], od_sem.at[n, h]
        )
        theirs = remote(
            stage.at[h, other], out.at[:, head_cols(core * HALF + h)], sem, (h,), sibling
        )
        return mine, theirs

    def out_start(stage, out, sem, n, h):
        for copy in out_copy(stage, out, sem, n, h):
            copy.start()

    def out_wait(stage, out, sem, n, h):
        for copy in out_copy(stage, out, sem, n, h):
            copy.wait()

    def step(h):
        norm_of = lambda ref, g: ref[g, pl.ds(h, 1), :]
        delta_of = lambda ref, g: ref[g, pl.ds(HALF + h, 1), :]
        q0, g0, q1, g1 = q_own[h, 0], g_own[h, 0], q_own[h, 1], g_own[h, 1]
        n0, d0 = norm_of(stats, 0), delta_of(stats, 0)
        n1, d1 = norm_of(stats, 1), delta_of(stats, 1)
        dq_add, dk_add, dv_add = pair(h, 0, q0, g0, n0, d0, query_pos(0))
        dq_acc[h, 0] = dq_add
        dk_acc[0] = dk_add
        dv_acc[0] = dv_add
        dq_add, dk_add, dv_add = pair(h, 0, q1, g1, n1, d1, query_pos(1))
        dq_acc[h, 1] = dq_add
        dk_acc[0] += dk_add
        dv_acc[0] += dv_add
        dq_add, dk_add, dv_add = pair(h, 1, q1, g1, n1, d1, query_pos(1))
        dq_acc[h, 1] += dq_add
        dk_acc[1] = dk_add
        dv_acc[1] = dv_add

        @pl.when(h == 0)
        def _():
            send_far_s.wait_recv()
            send_s.wait_recv()

        send_far_g(h).wait_recv()
        send_far_q(h).wait_recv()
        dq_add, dk_add, dv_add = pair(
            h,
            1,
            q_far[h],
            g_far[h],
            stats_far[pl.ds(h, 1), :],
            stats_far[pl.ds(HALF + h, 1), :],
            query_pos(4),
        )
        far_stage[h] = dq_add.astype(BF16)
        back_far(h).start()
        dk_acc[1] += dk_add
        dv_acc[1] += dv_add

        for g in range(2):
            send_g(h, g).wait_recv()
            send_q(h, g).wait_recv()
            qn, gn = q_next[h, g], g_next[h, g]
            nn, dn = norm_of(stats_next, g), delta_of(stats_next, g)
            first, dk_add, dv_add = pair(h, 0, qn, gn, nn, dn, query_pos(2 + g))
            dk_acc[0] += dk_add
            dv_acc[0] += dv_add
            second, dk_add, dv_add = pair(h, 1, qn, gn, nn, dn, query_pos(2 + g))
            dk_acc[1] += dk_add
            dv_acc[1] += dv_add
            next_stage[h, g] = (first + second).astype(BF16)
            back_next(h, g).start()

        for c in range(2):
            dk_stage[h, c] = (dk_acc[c] * score_scale).astype(BF16)
            dv_stage[h, c] = dv_acc[c].astype(BF16)
        out_start(dk_stage, dk_out, ok_sem, 0, h)
        out_start(dv_stage, dv_out, ov_sem, 1, h)

    over_heads(step)

    def finish(h):
        back_far(h).wait_recv()
        for g in range(2):
            back_next(h, g).wait_recv()
            total = dq_acc[h, g] + next_back[h, g].astype(F32)
            if g == 0:
                total = total + far_back[h].astype(F32)
            dq_stage[h, g] = (total * score_scale).T.astype(BF16)
        out_start(dq_stage, dq_out, oq_sem, 2, h)

    over_heads(finish)

    for copy in sq_copies:
        copy.wait_send()
    give_s.wait_send()
    send_s.wait_send()
    send_far_s.wait_send()

    def drain(h):
        give_g(h).wait_send()
        give_v(h).wait_send()
        give_q(h).wait_send()
        give_k(h).wait_send()
        for g in range(2):
            send_g(h, g).wait_send()
            send_q(h, g).wait_send()
            back_next(h, g).wait_send()
        send_far_g(h).wait_send()
        send_far_q(h).wait_send()
        back_far(h).wait_send()
        out_wait(dk_stage, dk_out, ok_sem, 0, h)
        out_wait(dv_stage, dv_out, ov_sem, 1, h)
        out_wait(dq_stage, dq_out, oq_sem, 2, h)

    over_heads(drain)


def local(q_raw, k_raw, values, out_grad, attn_out, log_norm, q_gain, k_gain, order):
    seq_count = lax.axis_size("seq")
    head_count = lax.axis_size("head")
    rows, columns = q_raw.shape
    any_spec = pl.BlockSpec(memory_space=pl.ANY)
    vmem_spec = pl.BlockSpec(memory_space=pltpu.VMEM)
    whole = pltpu.VMEM((rows, columns), BF16)
    halves = pltpu.VMEM((HALF, 2, ROWS, HD), BF16)
    single = pltpu.VMEM((HALF, ROWS, HD), BF16)
    flipped = pltpu.VMEM((HALF, 2, HD, ROWS), BF16)
    table = pltpu.VMEM((2, 2 * HALF, ROWS), F32)
    table_one = pltpu.VMEM((2 * HALF, ROWS), F32)
    acc = pltpu.VMEM((2, ROWS, HD), F32)
    sem = pltpu.SemaphoreType.DMA
    scratch = [whole] * 4
    scratch += [halves, halves, halves, halves, flipped, table]
    scratch += [single, single, table_one]
    scratch += [pltpu.VMEM((head_count, 8, ROWS), F32)]
    scratch += [halves, halves, table, single, single, table_one]
    scratch += [pltpu.VMEM((HALF, 2, HD, ROWS), F32), acc, acc]
    scratch += [flipped, flipped]
    scratch += [pltpu.VMEM((HALF, HD, ROWS), BF16), pltpu.VMEM((HALF, HD, ROWS), BF16)]
    scratch += [halves, halves, halves]
    scratch += [sem((4,)), sem((HALF,)), sem((HALF,)), sem((2, head_count))]
    scratch += [sem((2, HALF))] * 4 + [sem((2, 1))]
    scratch += [sem((2, HALF, 2))] * 2 + [sem((2, 1))]
    scratch += [sem((2, HALF))] * 2 + [sem((2, 1))]
    scratch += [sem((2, HALF, 2)), sem((2, HALF))]
    scratch += [sem((3, HALF))] + [sem((2, HALF))] * 3
    shape = jax.ShapeDtypeStruct((rows, columns), BF16)
    return pl.pallas_call(
        functools.partial(kernel, seq_count, head_count),
        out_shape=(shape, shape, shape),
        in_specs=[pl.BlockSpec(memory_space=pltpu.SMEM)] + [any_spec] * 5 + [vmem_spec] * 3,
        out_specs=(any_spec, any_spec, any_spec),
        scratch_shapes=scratch,
        compiler_params=pltpu.CompilerParams(
            collective_id=0, has_side_effects=True, vmem_limit_bytes=62 * 1024 * 1024
        ),
        cost_estimate=pl.CostEstimate(
            flops=10 * 32 * ROWS * ROWS * HD,
            bytes_accessed=8 * rows * columns * 2,
            transcendentals=32 * ROWS * ROWS,
        ),
    )(
        order,
        q_raw,
        k_raw,
        values,
        out_grad,
        attn_out,
        log_norm,
        q_gain.reshape(1, columns),
        k_gain.reshape(1, columns),
    )


def solution(mesh):
    placed = P("seq", "head")
    return jax.shard_map(
        local,
        mesh=mesh,
        in_specs=(placed,) * 5 + (P("head", "seq"), P("head"), P("head"), P()),
        out_specs=(placed, placed, placed),
        check_vma=False,
    )
```

```python
import functools

import jax
import jax.numpy as jnp
from jax import lax
from jax.experimental import pallas as pl
from jax.experimental.pallas import tpu as pltpu
from jax.sharding import PartitionSpec as P

EPSILON = 1e-06
LOG2E = 1.4426950408889634
MESH = pl.DeviceIdType.MESH
F32 = jnp.float32
BF16 = jnp.bfloat16
HALF = 4
BLK = 128
ROWS = 256
HD = 128

NT = (((1,), (1,)), ((), ()))
NN = (((1,), (0,)), ((), ()))


def dot(a, b, dims):
    return lax.dot_general(a, b, dims, preferred_element_type=F32)


def head_cols(head):
    return pl.ds(pl.multiple_of(head * HD, HD), HD)


def kernel(
    seq_count,
    head_count,
    order,
    q_hbm,
    k_hbm,
    v_hbm,
    g_hbm,
    o_hbm,
    norm_ref,
    q_gain,
    k_gain,
    dq_out,
    dk_out,
    dv_out,
    q_all,
    k_all,
    g_all,
    o_all,
    q_own,
    g_own,
    k_own,
    v_own,
    k_flip,
    stats,
    q_stage,
    k_stage,
    stats_stage,
    squares,
    q_next,
    g_next,
    stats_next,
    q_far,
    g_far,
    stats_far,
    dq_acc,
    dk_acc,
    dv_acc,
    next_stage,
    next_back,
    far_stage,
    far_back,
    dq_stage,
    dk_stage,
    dv_stage,
    load_sem,
    load_g_sem,
    load_v_sem,
    sq_sem,
    xg_sem,
    xv_sem,
    xq_sem,
    xk_sem,
    xs_sem,
    ng_sem,
    nq_sem,
    ns_sem,
    fg_sem,
    fq_sem,
    fs_sem,
    nb_sem,
    fb_sem,
    od_sem,
    oq_sem,
    ok_sem,
    ov_sem,
):
    seq = lax.axis_index("seq")
    head = lax.axis_index("head")
    chip = seq // 2
    core = seq % 2
    other = 1 - core
    chips = seq_count // 2
    width = head_count * q_hbm.shape[1]
    score_scale = HD ** (-0.5)

    sibling = (chip * 2 + other, head)
    prev = (((chip + chips - 1) % chips) * 2 + core, head)
    succ = (((chip + 1) % chips) * 2 + core, head)
    prev_far = (((chip + chips - 2) % chips) * 2 + core, head)
    succ_far = (((chip + 2) % chips) * 2 + core, head)

    def remote(src, dst, sem, idx, device):
        return pltpu.make_async_remote_copy(
            src_ref=src,
            dst_ref=dst,
            send_sem=sem.at[(0, *idx)],
            recv_sem=sem.at[(1, *idx)],
            device_id=device,
            device_id_type=MESH,
        )

    barrier = pltpu.get_barrier_semaphore()
    for device in (sibling, prev, succ, prev_far, succ_far):
        pl.semaphore_signal(barrier, inc=1, device_id=device, device_id_type=MESH)
    for n in range(1, head_count):
        pl.semaphore_signal(
            barrier, inc=1, device_id=(seq, (head + n) % head_count), device_id_type=MESH
        )

    loads = [
        pltpu.make_async_copy(src, dst, load_sem.at[n])
        for n, (src, dst) in enumerate(
            ((q_hbm, q_all), (k_hbm, k_all), (g_hbm, g_all), (o_hbm, o_all))
        )
    ]

    def load_g(h):
        return pltpu.make_async_copy(
            g_hbm.at[:, head_cols(core * HALF + h)], g_own.at[h, core], load_g_sem.at[h]
        )

    def load_v(h):
        return pltpu.make_async_copy(
            v_hbm.at[:, head_cols(core * HALF + h)], v_own.at[h, core], load_v_sem.at[h]
        )

    loads[0].start()
    loads[1].start()
    for h in range(HALF):
        load_g(h).start()
    loads[2].start()
    loads[3].start()
    for h in range(HALF):
        load_v(h).start()

    def row_sums(src):
        def add(h, total):
            block = src[:, head_cols(h)].astype(F32)
            return total + block * block

        total = lax.fori_loop(0, 2 * HALF, add, jnp.zeros((ROWS, HD), F32))
        return jnp.sum(total.T, axis=0, keepdims=True)

    loads[0].wait()
    loads[1].wait()
    squares[0, 0:1, :] = row_sums(q_all)
    squares[0, 1:2, :] = row_sums(k_all)
    pl.semaphore_wait(barrier, 5 + head_count - 1)

    def give_g(h):
        return remote(
            g_hbm.at[:, head_cols(other * HALF + h)], g_own.at[h, core], xg_sem, (h,), sibling
        )

    def give_v(h):
        return remote(
            v_hbm.at[:, head_cols(other * HALF + h)], v_own.at[h, core], xv_sem, (h,), sibling
        )

    def give_q(h):
        return remote(q_stage.at[h], q_own.at[h, core], xq_sem, (h,), sibling)

    def give_k(h):
        return remote(k_stage.at[h], k_own.at[h, core], xk_sem, (h,), sibling)

    give_s = remote(stats_stage, stats.at[core], xs_sem, (0,), sibling)

    def send_g(h, g):
        return remote(g_own.at[h, g], g_next.at[h, g], ng_sem, (h, g), prev)

    def send_q(h, g):
        return remote(q_own.at[h, g], q_next.at[h, g], nq_sem, (h, g), prev)

    send_s = remote(stats, stats_next, ns_sem, (0,), prev)

    def send_far_g(h):
        return remote(g_own.at[h, 0], g_far.at[h], fg_sem, (h,), prev_far)

    def send_far_q(h):
        return remote(q_own.at[h, 0], q_far.at[h], fq_sem, (h,), prev_far)

    send_far_s = remote(stats.at[0], stats_far, fs_sem, (0,), prev_far)

    def back_next(h, g):
        return remote(next_stage.at[h, g], next_back.at[h, g], nb_sem, (h, g), succ)

    def back_far(h):
        return remote(far_stage.at[h], far_back.at[h], fb_sem, (h,), succ_far)

    def over_heads(body, first=0, last=HALF):
        lax.fori_loop(first, last, lambda h, c: (body(h), c)[1], 0)

    def start_next(send, h, g):
        @pl.when(g + chip % 2 > 0)
        def _():
            send(h, g).start()

    def start_far(send, h, g):
        @pl.when(g == 0)
        def _():
            send(h).start()

    def pass_on(src, dst, sem, h):
        @pl.when(chip % 2 == 0)
        def _():
            remote(src.at[h], dst.at[h, 0], sem, (h, 0), succ).start()

    sq_copies = []
    for n in range(1, head_count):
        copy = remote(
            squares.at[0], squares.at[n], sq_sem, (n,), (seq, (head + n) % head_count)
        )
        copy.start()
        sq_copies.append(copy)

    over_heads(lambda h: give_g(h).start())

    def first_g(h):
        load_g(h).wait()
        start_far(send_far_g, h, core)
        start_next(send_g, h, core)

    over_heads(first_g)
    over_heads(lambda h: give_v(h).start())

    loads[2].wait()
    loads[3].wait()
    norm_rows = norm_ref[...] * LOG2E

    def delta_row(h):
        product = g_all[:, head_cols(h)].astype(F32) * o_all[:, head_cols(h)].astype(F32)
        return jnp.sum(product.T, axis=0, keepdims=True)

    first_half = core == 0
    stats[core, 0:HALF, :] = jnp.where(first_half, norm_rows[0:HALF], norm_rows[HALF:])
    stats_stage[0:HALF, :] = jnp.where(first_half, norm_rows[HALF:], norm_rows[0:HALF])
    for h in range(HALF):
        stats[core, HALF + h : HALF + h + 1, :] = delta_row(core * HALF + h)
        stats_stage[HALF + h : HALF + h + 1, :] = delta_row(other * HALF + h)
    give_s.start()

    def second_g(h):
        give_g(h).wait_recv()
        start_far(send_far_g, h, other)
        start_next(send_g, h, other)

    over_heads(second_g, 0, HALF // 2)

    for copy in sq_copies:
        copy.wait_recv()
    over_heads(second_g, HALF // 2)
    give_s.wait_recv()
    send_s.start()
    send_far_s.start()
    total = squares[0]
    for n in range(1, head_count):
        total = total + squares[n]
    scale = lax.rsqrt(total / width + EPSILON)
    q_scale = jnp.broadcast_to(scale[0:1, :], (HD, ROWS)).T
    k_scale = jnp.broadcast_to(scale[1:2, :], (HD, ROWS)).T

    def normed(src, scales, gain, h):
        return (src[:, head_cols(h)].astype(F32) * scales * gain[0:1, head_cols(h)]).astype(BF16)

    def norm_q(h):
        q_stage[h] = normed(q_all, q_scale, q_gain, other * HALF + h)
        give_q(h).start()
        q_own[h, core] = normed(q_all, q_scale, q_gain, core * HALF + h)

    over_heads(norm_q)

    def queue_q(h):
        start_far(send_far_q, h, core)
        start_next(send_q, h, core)
        give_q(h).wait_recv()
        start_far(send_far_q, h, other)
        start_next(send_q, h, other)

    over_heads(queue_q)

    def pass_g(h):
        send_far_g(h).wait_recv()
        pass_on(g_far, g_next, ng_sem, h)

    @pl.when(core == 0)
    def _():
        over_heads(pass_g)

    def norm_k(h):
        k_stage[h] = normed(k_all, k_scale, k_gain, other * HALF + h)
        give_k(h).start()
        mine = normed(k_all, k_scale, k_gain, core * HALF + h)
        k_own[h, core] = mine
        k_flip[h, core] = mine.T

    over_heads(norm_k)

    def ready_kv(h):
        give_k(h).wait_recv()
        k_flip[h, other] = k_own[h, other].T
        give_v(h).wait_recv()
        load_v(h).wait()

    over_heads(ready_kv)

    def group_of(step):
        return (chip * 2 + step) % seq_count

    def key_pos(c):
        group = group_of(c)
        row = lax.broadcasted_iota(jnp.int32, (ROWS, ROWS), 0)
        return row + jnp.where(row < BLK, order[2 * group] * BLK, order[2 * group + 1] * BLK - BLK)

    def query_pos(step):
        group = group_of(step)
        col = lax.broadcasted_iota(jnp.int32, (1, ROWS), 1)
        return col + jnp.where(col < BLK, order[2 * group] * BLK, order[2 * group + 1] * BLK - BLK)

    def pair(h, c, q, g, norm_row, delta, q_at):
        s = dot(k_own[h, c], q, NT)
        d = dot(v_own[h, c], g, NT)
        p = jnp.exp2(s * (score_scale * LOG2E) - norm_row)
        p = jnp.where(key_pos(c) <= q_at, p, 0.0)
        ds = (p * (d - delta)).astype(BF16)
        dv_add = dot(p.astype(BF16), g, NN)
        dk_add = dot(ds, q, NN)
        dq_add = dot(k_flip[h, c], ds, NN)
        return dq_add, dk_add, dv_add

    def out_copy(stage, out, sem, n, h):
        mine = pltpu.make_async_copy(
            stage.at[h, core], out.at[:, head_cols(core * HALF + h)], od_sem.at[n, h]
        )
        theirs = remote(
            stage.at[h, other], out.at[:, head_cols(core * HALF + h)], sem, (h,), sibling
        )
        return mine, theirs

    def out_start(stage, out, sem, n, h):
        for copy in out_copy(stage, out, sem, n, h):
            copy.start()

    def out_wait(stage, out, sem, n, h):
        for copy in out_copy(stage, out, sem, n, h):
            copy.wait()

    norm_of = lambda ref, g, h: ref[g, pl.ds(h, 1), :]
    delta_of = lambda ref, g, h: ref[g, pl.ds(HALF + h, 1), :]

    def own(h):
        q0, g0, q1, g1 = q_own[h, 0], g_own[h, 0], q_own[h, 1], g_own[h, 1]
        n0, d0 = norm_of(stats, 0, h), delta_of(stats, 0, h)
        n1, d1 = norm_of(stats, 1, h), delta_of(stats, 1, h)
        dq_add, dk_add, dv_add = pair(h, 0, q0, g0, n0, d0, query_pos(0))
        dq_acc[h, 0] = dq_add
        dk_acc[h, 0] = dk_add
        dv_acc[h, 0] = dv_add
        dq_add, dk_add, dv_add = pair(h, 0, q1, g1, n1, d1, query_pos(1))
        dq_acc[h, 1] = dq_add
        dk_acc[h, 0] += dk_add
        dv_acc[h, 0] += dv_add
        dq_add, dk_add, dv_add = pair(h, 1, q1, g1, n1, d1, query_pos(1))
        dq_acc[h, 1] += dq_add
        dk_acc[h, 1] = dk_add
        dv_acc[h, 1] = dv_add

        @pl.when(core == 1)
        def _():
            pass_g(h)

    over_heads(own)

    send_far_s.wait_recv()
    send_s.wait_recv()

    def step(h):
        send_far_q(h).wait_recv()
        pass_on(q_far, q_next, nq_sem, h)
        dq_add, dk_add, dv_add = pair(
            h,
            1,
            q_far[h],
            g_far[h],
            stats_far[pl.ds(h, 1), :],
            stats_far[pl.ds(HALF + h, 1), :],
            query_pos(4),
        )
        far_stage[h] = dq_add.astype(BF16)
        back_far(h).start()
        dk_acc[h, 1] += dk_add
        dv_acc[h, 1] += dv_add

        for g in (1, 0):
            send_g(h, g).wait_recv()
            send_q(h, g).wait_recv()
            qn, gn = q_next[h, g], g_next[h, g]
            nn, dn = norm_of(stats_next, g, h), delta_of(stats_next, g, h)
            first, dk_add, dv_add = pair(h, 0, qn, gn, nn, dn, query_pos(2 + g))
            dk_acc[h, 0] += dk_add
            dv_acc[h, 0] += dv_add
            second, dk_add, dv_add = pair(h, 1, qn, gn, nn, dn, query_pos(2 + g))
            dk_acc[h, 1] += dk_add
            dv_acc[h, 1] += dv_add
            next_stage[h, g] = (first + second).astype(BF16)
            back_next(h, g).start()

        for c in range(2):
            dk_stage[h, c] = (dk_acc[h, c] * score_scale).astype(BF16)
            dv_stage[h, c] = dv_acc[h, c].astype(BF16)
        out_start(dk_stage, dk_out, ok_sem, 0, h)
        out_start(dv_stage, dv_out, ov_sem, 1, h)

    over_heads(step)

    def finish(h):
        back_far(h).wait_recv()
        for g in (1, 0):
            back_next(h, g).wait_recv()
            total = dq_acc[h, g] + next_back[h, g].astype(F32)
            if g == 0:
                total = total + far_back[h].astype(F32)
            dq_stage[h, g] = (total * score_scale).T.astype(BF16)
        out_start(dq_stage, dq_out, oq_sem, 2, h)

    over_heads(finish)

    for copy in sq_copies:
        copy.wait_send()
    give_s.wait_send()
    send_s.wait_send()
    send_far_s.wait_send()

    def drain(h):
        give_g(h).wait_send()
        give_v(h).wait_send()
        give_q(h).wait_send()
        give_k(h).wait_send()
        for g in range(2):
            send_g(h, g).wait_send()
            send_q(h, g).wait_send()
            back_next(h, g).wait_send()
        send_far_g(h).wait_send()
        send_far_q(h).wait_send()
        back_far(h).wait_send()
        out_wait(dk_stage, dk_out, ok_sem, 0, h)
        out_wait(dv_stage, dv_out, ov_sem, 1, h)
        out_wait(dq_stage, dq_out, oq_sem, 2, h)

    over_heads(drain)


def store_kernel(*refs):
    ins, outs, (held, sem_in, sem_out) = refs[:3], refs[3:6], refs[6:]
    half = ROWS // 2
    parts = [(n, part) for n in range(3) for part in range(2)]

    def load(n, part):
        rows = pl.ds(part * half, half)
        return pltpu.make_async_copy(ins[n].at[rows], held.at[n, rows], sem_in.at[n, part])

    def save(n, part):
        rows = pl.ds(part * half, half)
        return pltpu.make_async_copy(held.at[n, rows], outs[n].at[rows], sem_out.at[n, part])

    for n, part in parts:
        load(n, part).start()
    for n, part in parts:
        load(n, part).wait()
        save(n, part).start()
    for n, part in parts:
        save(n, part).wait()


def store(grads, shape):
    any_spec = pl.BlockSpec(memory_space=pl.ANY)
    sem = pltpu.SemaphoreType.DMA
    return pl.pallas_call(
        store_kernel,
        out_shape=(shape,) * 3,
        in_specs=[any_spec] * 3,
        out_specs=(any_spec,) * 3,
        scratch_shapes=[pltpu.VMEM((3, *shape.shape), BF16), sem((3, 2)), sem((3, 2))],
        compiler_params=pltpu.CompilerParams(vmem_limit_bytes=62 * 1024 * 1024),
    )(*grads)


def local(q_raw, k_raw, values, out_grad, attn_out, log_norm, q_gain, k_gain, order):
    seq_count = lax.axis_size("seq")
    head_count = lax.axis_size("head")
    rows, columns = q_raw.shape
    any_spec = pl.BlockSpec(memory_space=pl.ANY)
    vmem_spec = pl.BlockSpec(memory_space=pltpu.VMEM)
    whole = pltpu.VMEM((rows, columns), BF16)
    halves = pltpu.VMEM((HALF, 2, ROWS, HD), BF16)
    single = pltpu.VMEM((HALF, ROWS, HD), BF16)
    flipped = pltpu.VMEM((HALF, 2, HD, ROWS), BF16)
    table = pltpu.VMEM((2, 2 * HALF, ROWS), F32)
    table_one = pltpu.VMEM((2 * HALF, ROWS), F32)
    acc = pltpu.VMEM((HALF, 2, ROWS, HD), F32)
    sem = pltpu.SemaphoreType.DMA
    scratch = [whole] * 4
    scratch += [halves, halves, halves, halves, flipped, table]
    scratch += [single, single, table_one]
    scratch += [pltpu.VMEM((head_count, 2, ROWS), F32)]
    scratch += [halves, halves, table, single, single, table_one]
    scratch += [pltpu.VMEM((HALF, 2, HD, ROWS), F32), acc, acc]
    scratch += [flipped, flipped]
    scratch += [pltpu.VMEM((HALF, HD, ROWS), BF16), pltpu.VMEM((HALF, HD, ROWS), BF16)]
    scratch += [halves, halves, halves]
    scratch += [sem((4,)), sem((HALF,)), sem((HALF,)), sem((2, head_count))]
    scratch += [sem((2, HALF))] * 4 + [sem((2, 1))]
    scratch += [sem((2, HALF, 2))] * 2 + [sem((2, 1))]
    scratch += [sem((2, HALF))] * 2 + [sem((2, 1))]
    scratch += [sem((2, HALF, 2)), sem((2, HALF))]
    scratch += [sem((3, HALF))] + [sem((2, HALF))] * 3
    shape = jax.ShapeDtypeStruct((rows, columns), BF16)
    grads = pl.pallas_call(
        functools.partial(kernel, seq_count, head_count),
        out_shape=(shape, shape, shape),
        in_specs=[pl.BlockSpec(memory_space=pltpu.SMEM)] + [any_spec] * 5 + [vmem_spec] * 3,
        out_specs=(any_spec, any_spec, any_spec),
        scratch_shapes=scratch,
        compiler_params=pltpu.CompilerParams(
            collective_id=0, has_side_effects=True, vmem_limit_bytes=62 * 1024 * 1024
        ),
        cost_estimate=pl.CostEstimate(
            flops=10 * 32 * ROWS * ROWS * HD,
            bytes_accessed=8 * rows * columns * 2,
            transcendentals=32 * ROWS * ROWS,
        ),
    )(
        order,
        q_raw,
        k_raw,
        values,
        out_grad,
        attn_out,
        log_norm,
        q_gain.reshape(1, columns),
        k_gain.reshape(1, columns),
    )
    return store(grads, shape)


def solution(mesh):
    placed = P("seq", "head")
    return jax.shard_map(
        local,
        mesh=mesh,
        in_specs=(placed,) * 5 + (P("head", "seq"), P("head"), P("head"), P()),
        out_specs=(placed, placed, placed),
        check_vma=False,
    )
```

```python
import functools

import jax
import jax.numpy as jnp
from jax import lax
from jax.experimental import pallas as pl
from jax.experimental.pallas import tpu as pltpu
from jax.sharding import PartitionSpec as P

EPSILON = 1e-06
LOG2E = 1.4426950408889634
MESH = pl.DeviceIdType.MESH
F32 = jnp.float32
BF16 = jnp.bfloat16
HALF = 4
BLK = 128
ROWS = 256
HD = 128

NT = (((1,), (1,)), ((), ()))
NN = (((1,), (0,)), ((), ()))


def dot(a, b, dims):
    return lax.dot_general(a, b, dims, preferred_element_type=F32)


def head_cols(head):
    return pl.ds(pl.multiple_of(head * HD, HD), HD)


def kernel(
    seq_count,
    head_count,
    order,
    q_hbm,
    k_hbm,
    v_hbm,
    g_hbm,
    o_hbm,
    norm_ref,
    q_gain,
    k_gain,
    dq_out,
    dk_out,
    dv_out,
    q_all,
    k_all,
    g_all,
    o_all,
    q_own,
    g_own,
    k_own,
    v_own,
    k_flip,
    stats,
    q_stage,
    k_stage,
    stats_stage,
    squares,
    q_next,
    g_next,
    stats_next,
    q_far,
    g_far,
    stats_far,
    dq_acc,
    dk_acc,
    dv_acc,
    next_stage,
    next_back,
    far_stage,
    far_back,
    dq_given,
    dk_stage,
    dv_stage,
    load_sem,
    load_g_sem,
    load_v_sem,
    sq_sem,
    xg_sem,
    xv_sem,
    xq_sem,
    xk_sem,
    xs_sem,
    ng_sem,
    nq_sem,
    ns_sem,
    fg_sem,
    fq_sem,
    fs_sem,
    nb_sem,
    fb_sem,
    oq_sem,
    ok_sem,
    ov_sem,
):
    seq = lax.axis_index("seq")
    head = lax.axis_index("head")
    chip = seq // 2
    core = seq % 2
    other = 1 - core
    chips = seq_count // 2
    width = head_count * q_hbm.shape[1]
    score_scale = HD ** (-0.5)

    sibling = (chip * 2 + other, head)
    prev = (((chip + chips - 1) % chips) * 2 + core, head)
    succ = (((chip + 1) % chips) * 2 + core, head)
    prev_far = (((chip + chips - 2) % chips) * 2 + core, head)
    succ_far = (((chip + 2) % chips) * 2 + core, head)

    def on_core(device, which):
        return (device[0] // 2 * 2 + which, head)

    def remote(src, dst, sem, idx, device, there=None):
        return pltpu.make_async_remote_copy(
            src_ref=src,
            dst_ref=dst,
            send_sem=sem.at[(0, *idx)],
            recv_sem=sem.at[(1, *(there or idx))],
            device_id=device,
            device_id_type=MESH,
        )

    barrier = pltpu.get_barrier_semaphore()

    def signal(sem, device):
        pl.semaphore_signal(sem, inc=1, device_id=device, device_id_type=MESH)

    for device in (sibling, succ, succ_far, on_core(prev, 0), on_core(prev, 1)):
        signal(barrier, device)

    @pl.when(core == 0)
    def _():
        signal(barrier, on_core(prev_far, 0))
        signal(barrier, on_core(prev_far, 1))

    for n in range(1, head_count):
        signal(barrier, (seq, (head + n) % head_count))

    loads = [
        pltpu.make_async_copy(src, dst, load_sem.at[n])
        for n, (src, dst) in enumerate(
            ((q_hbm, q_all), (k_hbm, k_all), (g_hbm, g_all), (o_hbm, o_all))
        )
    ]

    def load_g(h):
        return pltpu.make_async_copy(
            g_hbm.at[:, head_cols(core * HALF + h)], g_own.at[h, core], load_g_sem.at[h]
        )

    def load_v(h):
        return pltpu.make_async_copy(
            v_hbm.at[:, head_cols(core * HALF + h)], v_own.at[h, core], load_v_sem.at[h]
        )

    loads[0].start()
    loads[1].start()
    for h in range(HALF):
        load_g(h).start()
    loads[2].start()
    loads[3].start()
    for h in range(HALF):
        load_v(h).start()

    def row_sums(src):
        def add(h, total):
            block = src[:, head_cols(h)].astype(F32)
            return total + block * block

        total = lax.fori_loop(0, 2 * HALF, add, jnp.zeros((ROWS, HD), F32))
        return jnp.sum(total.T, axis=0, keepdims=True)

    loads[0].wait()
    loads[1].wait()
    squares[0, 0:1, :] = row_sums(q_all)
    squares[0, 1:2, :] = row_sums(k_all)
    pl.semaphore_wait(barrier, 6 + head_count - 1)

    def give_g(h):
        return remote(
            g_hbm.at[:, head_cols(other * HALF + h)], g_own.at[h, core], xg_sem, (h,), sibling
        )

    def give_v(h):
        return remote(
            v_hbm.at[:, head_cols(other * HALF + h)], v_own.at[h, core], xv_sem, (h,), sibling
        )

    def give_q(h):
        return remote(q_stage.at[h], q_own.at[h, core], xq_sem, (h,), sibling)

    def give_k(h):
        return remote(k_stage.at[h], k_own.at[h, core], xk_sem, (h,), sibling)

    give_s = remote(stats_stage, stats.at[core], xs_sem, (0,), sibling)

    def send_g(h, g):
        return remote(g_own.at[h, g], g_next.at[h, g], ng_sem, (h, g), prev)

    def send_q(h, g):
        return remote(q_own.at[h, g], q_next.at[h, g], nq_sem, (h, g), prev)

    send_s = remote(stats, stats_next, ns_sem, (0,), prev)

    def send_far_g(h):
        return remote(g_own.at[h, 0], g_far.at[h], fg_sem, (h,), prev_far)

    def send_far_q(h):
        return remote(q_own.at[h, 0], q_far.at[h], fq_sem, (h,), prev_far)

    send_far_s = remote(stats.at[0], stats_far, fs_sem, (0,), prev_far)

    def back_next(h, g):
        return remote(
            next_stage.at[h, g], next_back.at[h, core], nb_sem, (h, g), on_core(succ, g), (h, core)
        )

    def back_far(h):
        return remote(
            far_stage.at[h], far_back.at[h, core], fb_sem, (h, 0), on_core(succ_far, 0), (h, core)
        )

    def back_next_from(h, half):
        return remote(
            next_stage.at[h, 0], next_back.at[h, half], nb_sem, (h, 0), sibling, (h, half)
        )

    def back_far_from(h, half):
        return remote(far_stage.at[h], far_back.at[h, half], fb_sem, (h, 0), sibling, (h, half))

    def give_dq(h):
        return remote(dq_acc.at[h, other], dq_given.at[h], oq_sem, (h,), sibling)

    def over_heads(body, first=0, last=HALF):
        lax.fori_loop(first, last, lambda h, c: (body(h), c)[1], 0)

    def start_next(send, h, g):
        @pl.when(g + chip % 2 > 0)
        def _():
            send(h, g).start()

    def start_far(send, h, g):
        @pl.when(g == 0)
        def _():
            send(h).start()

    def pass_on(src, dst, sem, h):
        @pl.when(chip % 2 == 0)
        def _():
            remote(src.at[h], dst.at[h, 0], sem, (h, 0), succ).start()

    over_heads(lambda h: give_g(h).start())

    def first_g(h):
        load_g(h).wait()
        start_next(send_g, h, core)


    sq_copies = []
    for n in range(1, head_count):
        copy = remote(
            squares.at[0], squares.at[n], sq_sem, (n,), (seq, (head + n) % head_count)
        )
        copy.start()
        sq_copies.append(copy)

    over_heads(first_g)
    over_heads(lambda h: give_v(h).start())

    def second_g(h):
        give_g(h).wait_recv()
        start_next(send_g, h, other)

    over_heads(second_g)
    over_heads(lambda h: send_far_g(h).start())

    loads[2].wait()
    loads[3].wait()
    norm_rows = norm_ref[...] * LOG2E

    def delta_row(h):
        product = g_all[:, head_cols(h)].astype(F32) * o_all[:, head_cols(h)].astype(F32)
        return jnp.sum(product.T, axis=0, keepdims=True)

    first_half = core == 0
    stats[core, 0:HALF, :] = jnp.where(first_half, norm_rows[0:HALF], norm_rows[HALF:])
    stats_stage[0:HALF, :] = jnp.where(first_half, norm_rows[HALF:], norm_rows[0:HALF])
    for h in range(HALF):
        stats[core, HALF + h : HALF + h + 1, :] = delta_row(core * HALF + h)
        stats_stage[HALF + h : HALF + h + 1, :] = delta_row(other * HALF + h)
    give_s.start()

    for copy in sq_copies:
        copy.wait_recv()
    give_s.wait_recv()
    send_s.start()
    send_far_s.start()
    total = squares[0]
    for n in range(1, head_count):
        total = total + squares[n]
    scale = lax.rsqrt(total / width + EPSILON)
    q_scale = jnp.broadcast_to(scale[0:1, :], (HD, ROWS)).T
    k_scale = jnp.broadcast_to(scale[1:2, :], (HD, ROWS)).T

    def normed(src, scales, gain, h):
        return (src[:, head_cols(h)].astype(F32) * scales * gain[0:1, head_cols(h)]).astype(BF16)

    def norm_q(h):
        q_stage[h] = normed(q_all, q_scale, q_gain, other * HALF + h)
        give_q(h).start()
        q_own[h, core] = normed(q_all, q_scale, q_gain, core * HALF + h)

    over_heads(norm_q)

    def queue_far_q(h):
        @pl.when(core == 1)
        def _():
            give_q(h).wait_recv()

        send_far_q(h).start()

    def queue_q(h):
        start_next(send_q, h, core)

        @pl.when(core == 0)
        def _():
            give_q(h).wait_recv()

        start_next(send_q, h, other)

    over_heads(queue_far_q)
    over_heads(queue_q)

    def pass_g(h):
        send_far_g(h).wait_recv()
        pass_on(g_far, g_next, ng_sem, h)

    def norm_k(h):
        k_stage[h] = normed(k_all, k_scale, k_gain, other * HALF + h)
        give_k(h).start()
        mine = normed(k_all, k_scale, k_gain, core * HALF + h)
        k_own[h, core] = mine
        k_flip[h, core] = mine.T

    over_heads(norm_k)

    def ready_kv(h):
        give_k(h).wait_recv()
        k_flip[h, other] = k_own[h, other].T
        give_v(h).wait_recv()
        load_v(h).wait()

    over_heads(ready_kv)

    def group_of(step):
        return (chip * 2 + step) % seq_count

    def blocks_of(step):
        group = group_of(step)
        return order[2 * group], order[2 * group + 1]

    def pair(h, c, step, q, g, norm_row, delta):
        s = dot(k_own[h, c], q, NT)
        d = dot(v_own[h, c], g, NT)
        query_at, key_at = blocks_of(step), blocks_of(c)
        col = lax.broadcasted_iota(jnp.int32, (1, ROWS), 1)
        parts = []
        for half in range(2):
            scaled = s[half * BLK : (half + 1) * BLK] * (score_scale * LOG2E)
            if step == c:
                query_pos = jnp.where(
                    col < BLK, query_at[0] * BLK, query_at[1] * BLK - BLK
                ) + col
                key_pos = key_at[half] * BLK + lax.broadcasted_iota(jnp.int32, (BLK, ROWS), 0)
                part = jnp.where(key_pos <= query_pos, jnp.exp2(scaled - norm_row), 0.0)
            else:
                hidden = [jnp.where(key_at[half] > at, 1e30, 0.0) for at in query_at]
                part = jnp.exp2(scaled - (norm_row + jnp.where(col < BLK, hidden[0], hidden[1])))
            parts.append(part)
        p = jnp.concatenate(parts, axis=0)
        ds = (p * (d - delta)).astype(BF16)
        dv_add = dot(p.astype(BF16), g, NN)
        dk_add = dot(ds, q, NN)
        dq_add = dot(k_flip[h, c], ds, NN)
        return dq_add, dk_add, dv_add

    def out_copy(stage, out, sem, h):
        return remote(
            stage.at[h], out.at[:, head_cols(core * HALF + h)], sem, (h,), sibling
        )

    def put(value_of, stage, out, sem, h):
        stage[h] = value_of(other)
        out_copy(stage, out, sem, h).start()
        out[:, head_cols(core * HALF + h)] = value_of(core)

    norm_of = lambda ref, g, h: ref[g, pl.ds(h, 1), :]
    delta_of = lambda ref, g, h: ref[g, pl.ds(HALF + h, 1), :]

    def own(h):
        q0, g0, q1, g1 = q_own[h, 0], g_own[h, 0], q_own[h, 1], g_own[h, 1]
        n0, d0 = norm_of(stats, 0, h), delta_of(stats, 0, h)
        n1, d1 = norm_of(stats, 1, h), delta_of(stats, 1, h)
        dq_add, dk_add, dv_add = pair(h, 0, 0, q0, g0, n0, d0)
        dq_acc[h, 0] = dq_add
        dk_acc[h, 0] = dk_add
        dv_acc[h, 0] = dv_add
        dq_add, dk_add, dv_add = pair(h, 0, 1, q1, g1, n1, d1)
        dq_acc[h, 1] = dq_add
        dk_acc[h, 0] += dk_add
        dv_acc[h, 0] += dv_add
        dq_add, dk_add, dv_add = pair(h, 1, 1, q1, g1, n1, d1)
        dq_acc[h, 1] += dq_add
        dk_acc[h, 1] = dk_add
        dv_acc[h, 1] = dv_add
        give_dq(h).start()

        pass_g(h)

    over_heads(own)

    send_far_s.wait_recv()
    send_s.wait_recv()

    def step(h):
        send_far_q(h).wait_recv()
        pass_on(q_far, q_next, nq_sem, h)
        dq_add, dk_add, dv_add = pair(
            h,
            1,
            4,
            q_far[h],
            g_far[h],
            stats_far[pl.ds(h, 1), :],
            stats_far[pl.ds(HALF + h, 1), :],
        )
        far_stage[h] = dq_add.astype(BF16)
        back_far(h).start()
        dk_acc[h, 1] += dk_add
        dv_acc[h, 1] += dv_add

        for g in (1, 0):
            send_g(h, g).wait_recv()
            send_q(h, g).wait_recv()
            qn, gn = q_next[h, g], g_next[h, g]
            nn, dn = norm_of(stats_next, g, h), delta_of(stats_next, g, h)
            first, dk_add, dv_add = pair(h, 0, 2 + g, qn, gn, nn, dn)
            dk_acc[h, 0] += dk_add
            dv_acc[h, 0] += dv_add
            second, dk_add, dv_add = pair(h, 1, 2 + g, qn, gn, nn, dn)
            dk_acc[h, 1] += dk_add
            dv_acc[h, 1] += dv_add
            next_stage[h, g] = (first + second).astype(BF16)

            @pl.when(chip % 2 == 1)
            def _():
                back_next(h, g).start()

            @pl.when((chip % 2 == 0) & (h > 0))
            def _():
                back_next(h - 1, g).start()

            @pl.when((chip % 2 == 0) & (h == HALF - 1))
            def _():
                back_next(h, g).start()

        put(
            lambda c: (dk_acc[h, c] * score_scale).astype(BF16), dk_stage, dk_out, ok_sem, h
        )
        put(lambda c: dv_acc[h, c].astype(BF16), dv_stage, dv_out, ov_sem, h)

    over_heads(step)

    def finish(h):
        give_dq(h).wait_recv()
        for half, total in ((core, dq_acc.at[h, core]), (other, dq_given.at[h])):

            @pl.when(core == 0)
            def _():
                back_far_from(h, half).wait_recv()
                total[...] += far_back[h, half].astype(F32)

            back_next_from(h, half).wait_recv()
            grad = total[...] + next_back[h, half].astype(F32)
            dq_out[:, head_cols(half * HALF + h)] = (grad * score_scale).T.astype(BF16)

    over_heads(finish)

    for copy in sq_copies:
        copy.wait_send()
    give_s.wait_send()
    send_s.wait_send()
    send_far_s.wait_send()

    def drain(h):
        give_g(h).wait_send()
        give_v(h).wait_send()
        give_q(h).wait_send()
        give_k(h).wait_send()
        for g in range(2):
            send_g(h, g).wait_send()
            send_q(h, g).wait_send()
            back_next(h, g).wait_send()
        send_far_g(h).wait_send()
        send_far_q(h).wait_send()
        back_far(h).wait_send()
        out_copy(dk_stage, dk_out, ok_sem, h).wait()
        out_copy(dv_stage, dv_out, ov_sem, h).wait()
        give_dq(h).wait_send()

    over_heads(drain)


def store_kernel(*refs):
    ins, outs, sem = refs[:3], refs[3:6], refs[6]
    half = ROWS // 2
    copies = []
    for n in range(3):
        for part in range(2):
            rows = pl.ds(part * half, half)
            copies.append(
                pltpu.make_async_copy(ins[n].at[rows], outs[n].at[rows], sem.at[n, part])
            )
    for copy in copies:
        copy.start()
    for copy in copies:
        copy.wait()


def store(grads, shape):
    return pl.pallas_call(
        store_kernel,
        out_shape=(shape,) * 3,
        in_specs=[pl.BlockSpec(memory_space=pltpu.VMEM)] * 3,
        out_specs=(pl.BlockSpec(memory_space=pl.ANY),) * 3,
        scratch_shapes=[pltpu.SemaphoreType.DMA((3, 2))],
        compiler_params=pltpu.CompilerParams(vmem_limit_bytes=4 * 1024 * 1024),
    )(*grads)


def local(q_raw, k_raw, values, out_grad, attn_out, log_norm, q_gain, k_gain, order):
    seq_count = lax.axis_size("seq")
    head_count = lax.axis_size("head")
    rows, columns = q_raw.shape
    any_spec = pl.BlockSpec(memory_space=pl.ANY)
    vmem_spec = pl.BlockSpec(memory_space=pltpu.VMEM)
    whole = pltpu.VMEM((rows, columns), BF16)
    halves = pltpu.VMEM((HALF, 2, ROWS, HD), BF16)
    single = pltpu.VMEM((HALF, ROWS, HD), BF16)
    flipped = pltpu.VMEM((HALF, 2, HD, ROWS), BF16)
    table = pltpu.VMEM((2, 2 * HALF, ROWS), F32)
    table_one = pltpu.VMEM((2 * HALF, ROWS), F32)
    acc = pltpu.VMEM((HALF, 2, ROWS, HD), F32)
    sem = pltpu.SemaphoreType.DMA
    scratch = [whole] * 4
    scratch += [halves, halves, halves, halves, flipped, table]
    scratch += [single, single, table_one]
    scratch += [pltpu.VMEM((head_count, 2, ROWS), F32)]
    scratch += [halves, halves, table, single, single, table_one]
    scratch += [pltpu.VMEM((HALF, 2, HD, ROWS), F32), acc, acc]
    scratch += [flipped, flipped]
    scratch += [pltpu.VMEM((HALF, HD, ROWS), BF16), flipped]
    scratch += [pltpu.VMEM((HALF, HD, ROWS), F32), single, single]
    scratch += [sem((4,)), sem((HALF,)), sem((HALF,)), sem((2, head_count))]
    scratch += [sem((2, HALF))] * 4 + [sem((2, 1))]
    scratch += [sem((2, HALF, 2))] * 2 + [sem((2, 1))]
    scratch += [sem((2, HALF))] * 2 + [sem((2, 1))]
    scratch += [sem((2, HALF, 2)), sem((2, HALF, 2))]
    scratch += [sem((2, HALF))] * 3
    shape = jax.ShapeDtypeStruct((rows, columns), BF16)
    grads = pl.pallas_call(
        functools.partial(kernel, seq_count, head_count),
        out_shape=(whole,) * 3,
        in_specs=[pl.BlockSpec(memory_space=pltpu.SMEM)] + [any_spec] * 5 + [vmem_spec] * 3,
        out_specs=(vmem_spec,) * 3,
        scratch_shapes=scratch,
        compiler_params=pltpu.CompilerParams(
            collective_id=0, has_side_effects=True, vmem_limit_bytes=62 * 1024 * 1024
        ),
        cost_estimate=pl.CostEstimate(
            flops=10 * 32 * ROWS * ROWS * HD,
            bytes_accessed=8 * rows * columns * 2,
            transcendentals=32 * ROWS * ROWS,
        ),
    )(
        order,
        q_raw,
        k_raw,
        values,
        out_grad,
        attn_out,
        log_norm,
        q_gain.reshape(1, columns),
        k_gain.reshape(1, columns),
    )
    return store(grads, shape)


def solution(mesh):
    placed = P("seq", "head")
    return jax.shard_map(
        local,
        mesh=mesh,
        in_specs=(placed,) * 5 + (P("head", "seq"), P("head"), P("head"), P()),
        out_specs=(placed, placed, placed),
        check_vma=False,
    )
```

```python
import functools

import jax
import jax.numpy as jnp
from jax import lax
from jax.experimental import pallas as pl
from jax.experimental.pallas import tpu as pltpu
from jax.sharding import PartitionSpec as P

EPSILON = 1e-06
LOG2E = 1.4426950408889634
MESH = pl.DeviceIdType.MESH
F32 = jnp.float32
BF16 = jnp.bfloat16
HALF = 4
BLK = 128
ROWS = 256
HD = 128

NT = (((1,), (1,)), ((), ()))
NN = (((1,), (0,)), ((), ()))

def dot(a, b, dims):
    return lax.dot_general(a, b, dims, preferred_element_type=F32)

def head_cols(head):
    return pl.ds(pl.multiple_of(head * HD, HD), HD)

def kernel(
    seq_count,
    head_count,
    order,
    q_hbm,
    k_hbm,
    v_hbm,
    g_hbm,
    o_hbm,
    norm_ref,
    q_gain,
    k_gain,
    dq_out,
    dk_out,
    dv_out,
    q_all,
    k_all,
    g_all,
    o_all,
    q_own,
    g_own,
    k_own,
    v_own,
    k_flip,
    stats,
    q_stage,
    k_stage,
    stats_stage,
    squares,
    q_next,
    g_next,
    stats_next,
    q_far,
    g_far,
    stats_far,
    dq_acc,
    dk_acc,
    dv_acc,
    next_stage,
    next_back,
    far_stage,
    far_back,
    dq_given,
    dk_stage,
    dv_stage,
    load_sem,
    load_g_sem,
    load_v_sem,
    sq_sem,
    xg_sem,
    xv_sem,
    xq_sem,
    xk_sem,
    xs_sem,
    ng_sem,
    nq_sem,
    ns_sem,
    fg_sem,
    fq_sem,
    fs_sem,
    nb_sem,
    fb_sem,
    oq_sem,
    ok_sem,
    ov_sem,
):
    seq = lax.axis_index("seq")
    head = lax.axis_index("head")
    chip = seq // 2
    core = seq % 2
    other = 1 - core
    chips = seq_count // 2
    width = head_count * q_hbm.shape[1]
    score_scale = HD ** (-0.5)

    sibling = (chip * 2 + other, head)
    prev = (((chip + chips - 1) % chips) * 2 + core, head)
    succ = (((chip + 1) % chips) * 2 + core, head)
    prev_far = (((chip + chips - 2) % chips) * 2 + core, head)
    succ_far = (((chip + 2) % chips) * 2 + core, head)

    def on_core(device, which):
        return (device[0] // 2 * 2 + which, head)

    def remote(src, dst, sem, idx, device, there=None):
        return pltpu.make_async_remote_copy(
            src_ref=src,
            dst_ref=dst,
            send_sem=sem.at[(0, *idx)],
            recv_sem=sem.at[(1, *(there or idx))],
            device_id=device,
            device_id_type=MESH,
        )

    barrier = pltpu.get_barrier_semaphore()

    def signal(sem, device):
        pl.semaphore_signal(sem, inc=1, device_id=device, device_id_type=MESH)

    for device in (sibling, succ, succ_far, on_core(prev, 0), on_core(prev, 1)):
        signal(barrier, device)

    @pl.when(core == 0)
    def _():
        signal(barrier, on_core(prev_far, 0))
        signal(barrier, on_core(prev_far, 1))

    for n in range(1, head_count):
        signal(barrier, (seq, (head + n) % head_count))

    loads = [
        pltpu.make_async_copy(src, dst, load_sem.at[n])
        for n, (src, dst) in enumerate(
            ((q_hbm, q_all), (k_hbm, k_all), (g_hbm, g_all), (o_hbm, o_all))
        )
    ]

    def load_g(h):
        return pltpu.make_async_copy(
            g_hbm.at[:, head_cols(core * HALF + h)], g_own.at[h, core], load_g_sem.at[h]
        )

    def load_v(h):
        return pltpu.make_async_copy(
            v_hbm.at[:, head_cols(core * HALF + h)], v_own.at[h, core], load_v_sem.at[h]
        )

    for h in range(HALF):
        load_g(h).start()
    loads[0].start()
    loads[1].start()
    loads[2].start()
    loads[3].start()
    for h in range(HALF):
        load_v(h).start()

    pl.semaphore_wait(barrier, 6 + head_count - 1)

    def give_g(h):
        return remote(
            g_hbm.at[:, head_cols(other * HALF + h)], g_own.at[h, core], xg_sem, (h,), sibling
        )

    def give_v(h):
        return remote(
            v_hbm.at[:, head_cols(other * HALF + h)], v_own.at[h, core], xv_sem, (h,), sibling
        )

    def give_q(h):
        return remote(q_stage.at[h], q_own.at[h, core], xq_sem, (h,), sibling)

    def give_k(h):
        return remote(k_stage.at[h], k_own.at[h, core], xk_sem, (h,), sibling)

    give_s = remote(stats_stage, stats.at[core], xs_sem, (0,), sibling)

    def send_g(h, g):
        return remote(g_own.at[h, g], g_next.at[h, g], ng_sem, (h, g), prev)

    def send_q(h, g):
        return remote(q_own.at[h, g], q_next.at[h, g], nq_sem, (h, g), prev)

    send_s = remote(stats, stats_next, ns_sem, (0,), prev)

    def send_far_g(h):
        return remote(g_own.at[h, 0], g_far.at[h], fg_sem, (h,), prev_far)

    def send_far_q(h):
        return remote(q_own.at[h, 0], q_far.at[h], fq_sem, (h,), prev_far)

    send_far_s = remote(stats.at[0], stats_far, fs_sem, (0,), prev_far)

    def back_next(h, g):
        return remote(
            next_stage.at[h, g], next_back.at[h, core], nb_sem, (h, g), on_core(succ, g), (h, core)
        )

    def back_far(h):
        return remote(
            far_stage.at[h], far_back.at[h, core], fb_sem, (h, 0), on_core(succ_far, 0), (h, core)
        )

    def back_next_from(h, half):
        return remote(
            next_stage.at[h, 0], next_back.at[h, half], nb_sem, (h, 0), sibling, (h, half)
        )

    def back_far_from(h, half):
        return remote(far_stage.at[h], far_back.at[h, half], fb_sem, (h, 0), sibling, (h, half))

    def give_dq(h):
        return remote(dq_acc.at[h, other], dq_given.at[h], oq_sem, (h,), sibling)

    def over_heads(body, first=0, last=HALF):
        lax.fori_loop(first, last, lambda h, c: (body(h), c)[1], 0)

    def start_next(send, h, g):
        @pl.when(g + chip % 2 > 0)
        def _():
            send(h, g).start()

    def start_far(send, h, g):
        @pl.when(g == 0)
        def _():
            send(h).start()

    def pass_on(src, dst, sem, h):
        @pl.when(chip % 2 == 0)
        def _():
            remote(src.at[h], dst.at[h, 0], sem, (h, 0), succ).start()

    over_heads(lambda h: give_g(h).start())

    def first_g(h):
        load_g(h).wait()
        start_next(send_g, h, core)

    over_heads(first_g, 0, 1)

    def row_sums(src):
        def add(h, total):
            block = src[:, head_cols(h)].astype(F32)
            return total + block * block

        total = lax.fori_loop(0, 2 * HALF, add, jnp.zeros((ROWS, HD), F32))
        return jnp.sum(total.T, axis=0, keepdims=True)

    loads[0].wait()
    loads[1].wait()
    squares[0, 0:1, :] = row_sums(q_all)
    squares[0, 1:2, :] = row_sums(k_all)
    sq_copies = []
    for n in range(1, head_count):
        copy = remote(
            squares.at[0], squares.at[n], sq_sem, (n,), (seq, (head + n) % head_count)
        )
        copy.start()
        sq_copies.append(copy)

    over_heads(first_g, 1)
    over_heads(lambda h: give_v(h).start())

    def second_g(h):
        give_g(h).wait_recv()
        start_next(send_g, h, other)

    over_heads(second_g)
    over_heads(lambda h: send_far_g(h).start())

    loads[2].wait()
    loads[3].wait()
    norm_rows = norm_ref[...] * LOG2E

    def delta_row(h):
        product = g_all[:, head_cols(h)].astype(F32) * o_all[:, head_cols(h)].astype(F32)
        return jnp.sum(product.T, axis=0, keepdims=True)

    first_half = core == 0
    stats[core, 0:HALF, :] = jnp.where(first_half, norm_rows[0:HALF], norm_rows[HALF:])
    stats_stage[0:HALF, :] = jnp.where(first_half, norm_rows[HALF:], norm_rows[0:HALF])
    for h in range(HALF):
        stats[core, HALF + h : HALF + h + 1, :] = delta_row(core * HALF + h)
        stats_stage[HALF + h : HALF + h + 1, :] = delta_row(other * HALF + h)
    give_s.start()

    for copy in sq_copies:
        copy.wait_recv()
    give_s.wait_recv()
    send_s.start()
    send_far_s.start()
    total = squares[0]
    for n in range(1, head_count):
        total = total + squares[n]
    scale = lax.rsqrt(total / width + EPSILON)
    q_scale = jnp.broadcast_to(scale[0:1, :], (HD, ROWS)).T
    k_scale = jnp.broadcast_to(scale[1:2, :], (HD, ROWS)).T

    def normed(src, scales, gain, h):
        return (src[:, head_cols(h)].astype(F32) * scales * gain[0:1, head_cols(h)]).astype(BF16)

    def norm_q(h):
        q_stage[h] = normed(q_all, q_scale, q_gain, other * HALF + h)
        give_q(h).start()
        q_own[h, core] = normed(q_all, q_scale, q_gain, core * HALF + h)

    over_heads(norm_q)

    def queue_far_q(h):
        @pl.when(core == 1)
        def _():
            give_q(h).wait_recv()

        send_far_q(h).start()

    def queue_q(h):
        start_next(send_q, h, core)

        @pl.when(core == 0)
        def _():
            give_q(h).wait_recv()

        start_next(send_q, h, other)

    over_heads(queue_far_q)
    over_heads(queue_q)

    def pass_g(h):
        send_far_g(h).wait_recv()
        pass_on(g_far, g_next, ng_sem, h)

    def norm_k(h):
        k_stage[h] = normed(k_all, k_scale, k_gain, other * HALF + h)
        give_k(h).start()
        mine = normed(k_all, k_scale, k_gain, core * HALF + h)
        k_own[h, core] = mine
        k_flip[h, core] = mine.T

    over_heads(norm_k)

    def ready_kv(h):
        give_k(h).wait_recv()
        k_flip[h, other] = k_own[h, other].T
        give_v(h).wait_recv()
        load_v(h).wait()

    over_heads(ready_kv)

    def group_of(step):
        return (chip * 2 + step) % seq_count

    def blocks_of(step):
        group = group_of(step)
        return order[2 * group], order[2 * group + 1]

    def pair(h, c, step, q, g, norm_row, delta):
        s = dot(k_own[h, c], q, NT)
        d = dot(v_own[h, c], g, NT)
        query_at, key_at = blocks_of(step), blocks_of(c)
        col = lax.broadcasted_iota(jnp.int32, (1, ROWS), 1)
        parts = []
        for half in range(2):
            scaled = s[half * BLK : (half + 1) * BLK] * (score_scale * LOG2E)
            if isinstance(step, int) and step == c:
                query_pos = jnp.where(
                    col < BLK, query_at[0] * BLK, query_at[1] * BLK - BLK
                ) + col
                key_pos = key_at[half] * BLK + lax.broadcasted_iota(jnp.int32, (BLK, ROWS), 0)
                part = jnp.where(key_pos <= query_pos, jnp.exp2(scaled - norm_row), 0.0)
            else:
                hidden = [jnp.where(key_at[half] > at, 1e30, 0.0) for at in query_at]
                part = jnp.exp2(scaled - (norm_row + jnp.where(col < BLK, hidden[0], hidden[1])))
            parts.append(part)
        p = jnp.concatenate(parts, axis=0)
        ds = (p * (d - delta)).astype(BF16)
        dv_add = dot(p.astype(BF16), g, NN)
        dk_add = dot(ds, q, NN)
        dq_add = dot(k_flip[h, c], ds, NN)
        return dq_add, dk_add, dv_add

    def out_copy(stage, out, sem, h):
        return remote(
            stage.at[h], out.at[:, head_cols(core * HALF + h)], sem, (h,), sibling
        )

    def put(value_of, stage, out, sem, h):
        stage[h] = value_of(other)
        out_copy(stage, out, sem, h).start()
        out[:, head_cols(core * HALF + h)] = value_of(core)

    norm_of = lambda ref, g, h: ref[g, pl.ds(h, 1), :]
    delta_of = lambda ref, g, h: ref[g, pl.ds(HALF + h, 1), :]

    def own(h):
        q0, g0, q1, g1 = q_own[h, 0], g_own[h, 0], q_own[h, 1], g_own[h, 1]
        n0, d0 = norm_of(stats, 0, h), delta_of(stats, 0, h)
        n1, d1 = norm_of(stats, 1, h), delta_of(stats, 1, h)
        dq_add, dk_add, dv_add = pair(h, 0, 0, q0, g0, n0, d0)
        dq_acc[h, 0] = dq_add
        dk_acc[h, 0] = dk_add
        dv_acc[h, 0] = dv_add
        dq_add, dk_add, dv_add = pair(h, 0, 1, q1, g1, n1, d1)
        dq_acc[h, 1] = dq_add
        dk_acc[h, 0] += dk_add
        dv_acc[h, 0] += dv_add
        dq_add, dk_add, dv_add = pair(h, 1, 1, q1, g1, n1, d1)
        dq_acc[h, 1] += dq_add
        dk_acc[h, 1] = dk_add
        dv_acc[h, 1] = dv_add
        give_dq(h).start()

        pass_g(h)

    over_heads(own)

    send_far_s.wait_recv()
    send_s.wait_recv()

    def far_step(h):
        send_far_q(h).wait_recv()
        pass_on(q_far, q_next, nq_sem, h)
        dq_add, dk_add, dv_add = pair(
            h,
            1,
            4,
            q_far[h],
            g_far[h],
            stats_far[pl.ds(h, 1), :],
            stats_far[pl.ds(HALF + h, 1), :],
        )
        far_stage[h] = dq_add.astype(BF16)
        back_far(h).start()
        dk_acc[h, 1] += dk_add
        dv_acc[h, 1] += dv_add

    over_heads(far_step)

    first_in = jnp.where(chip % 2 == 1, 0, core)

    def step(h):
        def next_group(n, carry):
            g = lax.rem(first_in + n, 2)
            send_g(h, g).wait_recv()
            send_q(h, g).wait_recv()
            qn, gn = q_next[h, g], g_next[h, g]
            nn, dn = norm_of(stats_next, g, h), delta_of(stats_next, g, h)
            first, dk_add, dv_add = pair(h, 0, 2 + g, qn, gn, nn, dn)
            dk_acc[h, 0] += dk_add
            dv_acc[h, 0] += dv_add
            second, dk_add, dv_add = pair(h, 1, 2 + g, qn, gn, nn, dn)
            dk_acc[h, 1] += dk_add
            dv_acc[h, 1] += dv_add
            next_stage[h, g] = (first + second).astype(BF16)

            back_next(h, g).start()
            return carry

        lax.fori_loop(0, 2, next_group, 0)

        put(
            lambda c: (dk_acc[h, c] * score_scale).astype(BF16), dk_stage, dk_out, ok_sem, h
        )
        put(lambda c: dv_acc[h, c].astype(BF16), dv_stage, dv_out, ov_sem, h)

    over_heads(step)

    def finish(h):
        give_dq(h).wait_recv()
        for half, total in ((core, dq_acc.at[h, core]), (other, dq_given.at[h])):

            @pl.when(core == 0)
            def _():
                back_far_from(h, half).wait_recv()
                total[...] += far_back[h, half].astype(F32)

            back_next_from(h, half).wait_recv()
            grad = total[...] + next_back[h, half].astype(F32)
            dq_out[:, head_cols(half * HALF + h)] = (grad * score_scale).T.astype(BF16)

    over_heads(finish)

    for copy in sq_copies:
        copy.wait_send()
    give_s.wait_send()
    send_s.wait_send()
    send_far_s.wait_send()

    def drain(h):
        give_g(h).wait_send()
        give_v(h).wait_send()
        give_q(h).wait_send()
        give_k(h).wait_send()
        for g in range(2):
            send_g(h, g).wait_send()
            send_q(h, g).wait_send()
            back_next(h, g).wait_send()
        send_far_g(h).wait_send()
        send_far_q(h).wait_send()
        back_far(h).wait_send()
        out_copy(dk_stage, dk_out, ok_sem, h).wait()
        out_copy(dv_stage, dv_out, ov_sem, h).wait()
        give_dq(h).wait_send()

    over_heads(drain)

def store_kernel(*refs):
    ins, outs, sem = refs[:3], refs[3:6], refs[6]
    half = ROWS // 2
    copies = []
    for n in range(3):
        for part in range(2):
            rows = pl.ds(part * half, half)
            copies.append(
                pltpu.make_async_copy(ins[n].at[rows], outs[n].at[rows], sem.at[n, part])
            )
    for copy in copies:
        copy.start()
    for copy in copies:
        copy.wait()

def store(grads, shape):
    return pl.pallas_call(
        store_kernel,
        out_shape=(shape,) * 3,
        in_specs=[pl.BlockSpec(memory_space=pltpu.VMEM)] * 3,
        out_specs=(pl.BlockSpec(memory_space=pl.ANY),) * 3,
        scratch_shapes=[pltpu.SemaphoreType.DMA((3, 2))],
        compiler_params=pltpu.CompilerParams(vmem_limit_bytes=4 * 1024 * 1024),
    )(*grads)

def local(q_raw, k_raw, values, out_grad, attn_out, log_norm, q_gain, k_gain, order):
    seq_count = lax.axis_size("seq")
    head_count = lax.axis_size("head")
    rows, columns = q_raw.shape
    any_spec = pl.BlockSpec(memory_space=pl.ANY)
    vmem_spec = pl.BlockSpec(memory_space=pltpu.VMEM)
    whole = pltpu.VMEM((rows, columns), BF16)
    halves = pltpu.VMEM((HALF, 2, ROWS, HD), BF16)
    single = pltpu.VMEM((HALF, ROWS, HD), BF16)
    flipped = pltpu.VMEM((HALF, 2, HD, ROWS), BF16)
    table = pltpu.VMEM((2, 2 * HALF, ROWS), F32)
    table_one = pltpu.VMEM((2 * HALF, ROWS), F32)
    acc = pltpu.VMEM((HALF, 2, ROWS, HD), F32)
    sem = pltpu.SemaphoreType.DMA
    scratch = [whole] * 4
    scratch += [halves, halves, halves, halves, flipped, table]
    scratch += [single, single, table_one]
    scratch += [pltpu.VMEM((head_count, 2, ROWS), F32)]
    scratch += [halves, halves, table, single, single, table_one]
    scratch += [pltpu.VMEM((HALF, 2, HD, ROWS), F32), acc, acc]
    scratch += [flipped, flipped]
    scratch += [pltpu.VMEM((HALF, HD, ROWS), BF16), flipped]
    scratch += [pltpu.VMEM((HALF, HD, ROWS), F32), single, single]
    scratch += [sem((4,)), sem((HALF,)), sem((HALF,)), sem((2, head_count))]
    scratch += [sem((2, HALF))] * 4 + [sem((2, 1))]
    scratch += [sem((2, HALF, 2))] * 2 + [sem((2, 1))]
    scratch += [sem((2, HALF))] * 2 + [sem((2, 1))]
    scratch += [sem((2, HALF, 2)), sem((2, HALF, 2))]
    scratch += [sem((2, HALF))] * 3
    shape = jax.ShapeDtypeStruct((rows, columns), BF16)
    grads = pl.pallas_call(
        functools.partial(kernel, seq_count, head_count),
        out_shape=(whole,) * 3,
        in_specs=[pl.BlockSpec(memory_space=pltpu.SMEM)] + [any_spec] * 5 + [vmem_spec] * 3,
        out_specs=(vmem_spec,) * 3,
        scratch_shapes=scratch,
        compiler_params=pltpu.CompilerParams(
            collective_id=0, has_side_effects=True, vmem_limit_bytes=62 * 1024 * 1024
        ),
        cost_estimate=pl.CostEstimate(
            flops=10 * 32 * ROWS * ROWS * HD,
            bytes_accessed=8 * rows * columns * 2,
            transcendentals=32 * ROWS * ROWS,
        ),
    )(
        order,
        q_raw,
        k_raw,
        values,
        out_grad,
        attn_out,
        log_norm,
        q_gain.reshape(1, columns),
        k_gain.reshape(1, columns),
    )
    return store(grads, shape)

def solution(mesh):
    placed = P("seq", "head")
    return jax.shard_map(
        local,
        mesh=mesh,
        in_specs=(placed,) * 5 + (P("head", "seq"), P("head"), P("head"), P()),
        out_specs=(placed, placed, placed),
        check_vma=False,
    )
```

```python
import functools

import jax
import jax.numpy as jnp
from jax import lax
from jax.experimental import pallas as pl
from jax.experimental.pallas import tpu as pltpu
from jax.sharding import PartitionSpec as P

EPSILON = 1e-06
LOG2E = 1.4426950408889634
MESH = pl.DeviceIdType.MESH
F32 = jnp.float32
BF16 = jnp.bfloat16
HALF = 4
BLK = 128
ROWS = 256
HD = 128

NT = (((1,), (1,)), ((), ()))
NN = (((1,), (0,)), ((), ()))

def dot(a, b, dims):
    return lax.dot_general(a, b, dims, preferred_element_type=F32)

def head_cols(head):
    return pl.ds(pl.multiple_of(head * HD, HD), HD)

def kernel(
    seq_count,
    head_count,
    order,
    q_hbm,
    k_hbm,
    v_hbm,
    g_hbm,
    o_hbm,
    norm_ref,
    q_gain,
    k_gain,
    dq_out,
    dk_out,
    dv_out,
    q_all,
    k_all,
    g_all,
    o_all,
    q_own,
    g_own,
    k_own,
    v_own,
    k_flip,
    stats,
    q_stage,
    k_stage,
    stats_stage,
    squares,
    q_next,
    g_next,
    stats_next,
    q_far,
    g_far,
    stats_far,
    dq_acc,
    dk_acc,
    dv_acc,
    next_stage,
    next_back,
    far_stage,
    far_back,
    dq_given,
    dk_stage,
    dv_stage,
    load_sem,
    load_g_sem,
    load_v_sem,
    sq_sem,
    xg_sem,
    xv_sem,
    xq_sem,
    xk_sem,
    xs_sem,
    ng_sem,
    nq_sem,
    ns_sem,
    fg_sem,
    fq_sem,
    fs_sem,
    nb_sem,
    fb_sem,
    oq_sem,
    ok_sem,
    ov_sem,
):
    seq = lax.axis_index("seq")
    head = lax.axis_index("head")
    chip = seq // 2
    core = seq % 2
    other = 1 - core
    chips = seq_count // 2
    width = head_count * q_hbm.shape[1]
    score_scale = HD ** (-0.5)

    sibling = (chip * 2 + other, head)
    prev = (((chip + chips - 1) % chips) * 2 + core, head)
    succ = (((chip + 1) % chips) * 2 + core, head)
    prev_far = (((chip + chips - 2) % chips) * 2 + core, head)
    succ_far = (((chip + 2) % chips) * 2 + core, head)

    def on_core(device, which):
        return (device[0] // 2 * 2 + which, head)

    def remote(src, dst, sem, idx, device, there=None):
        return pltpu.make_async_remote_copy(
            src_ref=src,
            dst_ref=dst,
            send_sem=sem.at[(0, *idx)],
            recv_sem=sem.at[(1, *(there or idx))],
            device_id=device,
            device_id_type=MESH,
        )

    barrier = pltpu.get_barrier_semaphore()

    def signal(sem, device):
        pl.semaphore_signal(sem, inc=1, device_id=device, device_id_type=MESH)

    for device in (sibling, succ, succ_far, on_core(prev, 0), on_core(prev, 1)):
        signal(barrier, device)

    @pl.when(core == 0)
    def _():
        signal(barrier, on_core(prev_far, 0))
        signal(barrier, on_core(prev_far, 1))

    for n in range(1, head_count):
        signal(barrier, (seq, (head + n) % head_count))

    loads = [
        pltpu.make_async_copy(src, dst, load_sem.at[n])
        for n, (src, dst) in enumerate(
            ((q_hbm, q_all), (k_hbm, k_all), (g_hbm, g_all), (o_hbm, o_all))
        )
    ]

    def load_g(h):
        return pltpu.make_async_copy(
            g_hbm.at[:, head_cols(core * HALF + h)], g_own.at[h, core], load_g_sem.at[h]
        )

    def load_v(h):
        return pltpu.make_async_copy(
            v_hbm.at[:, head_cols(core * HALF + h)], v_own.at[h, core], load_v_sem.at[h]
        )

    for h in range(HALF):
        load_g(h).start()
    loads[0].start()
    loads[1].start()
    loads[2].start()
    loads[3].start()
    for h in range(HALF):
        load_v(h).start()

    def row_sums(src):
        def add(h, total):
            block = src[:, head_cols(h)].astype(F32)
            return total + block * block

        total = lax.fori_loop(0, 2 * HALF, add, jnp.zeros((ROWS, HD), F32))
        return jnp.sum(total.T, axis=0, keepdims=True)

    def sum_squares():
        loads[0].wait()
        loads[1].wait()
        squares[0, 0:1, :] = row_sums(q_all)
        squares[0, 1:2, :] = row_sums(k_all)

    def make_stats():
        loads[2].wait()
        loads[3].wait()
        norm_rows = norm_ref[...] * LOG2E

        def delta_row(h):
            product = g_all[:, head_cols(h)].astype(F32) * o_all[:, head_cols(h)].astype(F32)
            return jnp.sum(product.T, axis=0, keepdims=True)

        first_half = core == 0
        stats[core, 0:HALF, :] = jnp.where(first_half, norm_rows[0:HALF], norm_rows[HALF:])
        stats_stage[0:HALF, :] = jnp.where(first_half, norm_rows[HALF:], norm_rows[0:HALF])
        for h in range(HALF):
            stats[core, HALF + h : HALF + h + 1, :] = delta_row(core * HALF + h)
            stats_stage[HALF + h : HALF + h + 1, :] = delta_row(other * HALF + h)

    sum_squares()
    make_stats()

    pl.semaphore_wait(barrier, 6 + head_count - 1)

    def give_g(h):
        return remote(
            g_hbm.at[:, head_cols(other * HALF + h)], g_own.at[h, core], xg_sem, (h,), sibling
        )

    def give_v(h):
        return remote(
            v_hbm.at[:, head_cols(other * HALF + h)], v_own.at[h, core], xv_sem, (h,), sibling
        )

    def give_q(h):
        return remote(q_stage.at[h], q_own.at[h, core], xq_sem, (h,), sibling)

    def give_k(h):
        return remote(k_stage.at[h], k_own.at[h, core], xk_sem, (h,), sibling)

    give_s = remote(stats_stage, stats.at[core], xs_sem, (0,), sibling)

    def send_g(h, g):
        return remote(g_own.at[h, g], g_next.at[h, g], ng_sem, (h, g), prev)

    def send_q(h, g):
        return remote(q_own.at[h, g], q_next.at[h, g], nq_sem, (h, g), prev)

    send_s = remote(stats, stats_next, ns_sem, (0,), prev)

    def send_far_g(h):
        return remote(g_own.at[h, 0], g_far.at[h], fg_sem, (h,), prev_far)

    def send_far_q(h):
        return remote(q_own.at[h, 0], q_far.at[h], fq_sem, (h,), prev_far)

    send_far_s = remote(stats.at[0], stats_far, fs_sem, (0,), prev_far)

    def back_next(h, g):
        return remote(
            next_stage.at[h, g], next_back.at[h, core], nb_sem, (h, g), on_core(succ, g), (h, core)
        )

    def back_far(h):
        return remote(
            far_stage.at[h], far_back.at[h, core], fb_sem, (h, 0), on_core(succ_far, 0), (h, core)
        )

    def back_next_from(h, half):
        return remote(
            next_stage.at[h, 0], next_back.at[h, half], nb_sem, (h, 0), sibling, (h, half)
        )

    def back_far_from(h, half):
        return remote(far_stage.at[h], far_back.at[h, half], fb_sem, (h, 0), sibling, (h, half))

    def give_dq(h):
        return remote(dq_acc.at[h, other], dq_given.at[h], oq_sem, (h,), sibling)

    def over_heads(body, first=0, last=HALF):
        lax.fori_loop(first, last, lambda h, c: (body(h), c)[1], 0)

    def start_next(send, h, g):
        @pl.when(g + chip % 2 > 0)
        def _():
            send(h, g).start()

    def start_far(send, h, g):
        @pl.when(g == 0)
        def _():
            send(h).start()

    def pass_on(src, dst, sem, h):
        @pl.when(chip % 2 == 0)
        def _():
            remote(src.at[h], dst.at[h, 0], sem, (h, 0), succ).start()

    def first_g(h):
        load_g(h).wait()
        start_next(send_g, h, core)

    sq_copies = []
    for n in range(1, head_count):
        copy = remote(
            squares.at[0], squares.at[n], sq_sem, (n,), (seq, (head + n) % head_count)
        )
        copy.start()
        sq_copies.append(copy)

    give_s.start()
    over_heads(lambda h: give_g(h).start())
    over_heads(first_g)
    over_heads(lambda h: give_v(h).start())

    def second_g(h):
        give_g(h).wait_recv()
        start_next(send_g, h, other)

    over_heads(second_g)
    over_heads(lambda h: send_far_g(h).start())

    for copy in sq_copies:
        copy.wait_recv()
    give_s.wait_recv()
    send_s.start()
    send_far_s.start()
    total = squares[0]
    for n in range(1, head_count):
        total = total + squares[n]
    scale = lax.rsqrt(total / width + EPSILON)
    q_scale = jnp.broadcast_to(scale[0:1, :], (HD, ROWS)).T
    k_scale = jnp.broadcast_to(scale[1:2, :], (HD, ROWS)).T

    def normed(src, scales, gain, h):
        return (src[:, head_cols(h)].astype(F32) * scales * gain[0:1, head_cols(h)]).astype(BF16)

    def norm_q(h):
        q_stage[h] = normed(q_all, q_scale, q_gain, other * HALF + h)
        give_q(h).start()
        q_own[h, core] = normed(q_all, q_scale, q_gain, core * HALF + h)

    over_heads(norm_q)

    def queue_far_q(h):
        @pl.when(core == 1)
        def _():
            give_q(h).wait_recv()

        send_far_q(h).start()

    def queue_q(h):
        start_next(send_q, h, core)

        @pl.when(core == 0)
        def _():
            give_q(h).wait_recv()

        start_next(send_q, h, other)

    over_heads(queue_far_q)
    over_heads(queue_q)

    def pass_g(h):
        send_far_g(h).wait_recv()
        pass_on(g_far, g_next, ng_sem, h)

    def norm_k(h):
        k_stage[h] = normed(k_all, k_scale, k_gain, other * HALF + h)
        give_k(h).start()
        mine = normed(k_all, k_scale, k_gain, core * HALF + h)
        k_own[h, core] = mine
        k_flip[h, core] = mine.T

    over_heads(norm_k)

    def ready_kv(h):
        give_k(h).wait_recv()
        k_flip[h, other] = k_own[h, other].T
        give_v(h).wait_recv()
        load_v(h).wait()

    over_heads(ready_kv)

    def group_of(step):
        return (chip * 2 + step) % seq_count

    def blocks_of(step):
        group = group_of(step)
        return order[2 * group], order[2 * group + 1]

    def pair(h, c, step, q, g, norm_row, delta):
        s = dot(k_own[h, c], q, NT)
        d = dot(v_own[h, c], g, NT)
        query_at, key_at = blocks_of(step), blocks_of(c)
        col = lax.broadcasted_iota(jnp.int32, (1, ROWS), 1)
        parts = []
        for half in range(2):
            scaled = s[half * BLK : (half + 1) * BLK] * (score_scale * LOG2E)
            if isinstance(step, int) and step == c:
                query_pos = jnp.where(
                    col < BLK, query_at[0] * BLK, query_at[1] * BLK - BLK
                ) + col
                key_pos = key_at[half] * BLK + lax.broadcasted_iota(jnp.int32, (BLK, ROWS), 0)
                part = jnp.where(key_pos <= query_pos, jnp.exp2(scaled - norm_row), 0.0)
            else:
                hidden = [jnp.where(key_at[half] > at, 1e30, 0.0) for at in query_at]
                part = jnp.exp2(scaled - (norm_row + jnp.where(col < BLK, hidden[0], hidden[1])))
            parts.append(part)
        p = jnp.concatenate(parts, axis=0)
        ds = (p * (d - delta)).astype(BF16)
        dv_add = dot(p.astype(BF16), g, NN)
        dk_add = dot(ds, q, NN)
        dq_add = dot(k_flip[h, c], ds, NN)
        return dq_add, dk_add, dv_add

    def out_copy(stage, out, sem, h):
        return remote(
            stage.at[h], out.at[:, head_cols(core * HALF + h)], sem, (h,), sibling
        )

    def put(value_of, stage, out, sem, h):
        stage[h] = value_of(other)
        out_copy(stage, out, sem, h).start()
        out[:, head_cols(core * HALF + h)] = value_of(core)

    norm_of = lambda ref, g, h: ref[g, pl.ds(h, 1), :]
    delta_of = lambda ref, g, h: ref[g, pl.ds(HALF + h, 1), :]

    def own(h):
        q0, g0, q1, g1 = q_own[h, 0], g_own[h, 0], q_own[h, 1], g_own[h, 1]
        n0, d0 = norm_of(stats, 0, h), delta_of(stats, 0, h)
        n1, d1 = norm_of(stats, 1, h), delta_of(stats, 1, h)
        dq_add, dk_add, dv_add = pair(h, 0, 0, q0, g0, n0, d0)
        dq_acc[h, 0] = dq_add
        dk_acc[h, 0] = dk_add
        dv_acc[h, 0] = dv_add
        dq_add, dk_add, dv_add = pair(h, 0, 1, q1, g1, n1, d1)
        dq_acc[h, 1] = dq_add
        dk_acc[h, 0] += dk_add
        dv_acc[h, 0] += dv_add
        dq_add, dk_add, dv_add = pair(h, 1, 1, q1, g1, n1, d1)
        dq_acc[h, 1] += dq_add
        dk_acc[h, 1] = dk_add
        dv_acc[h, 1] = dv_add
        give_dq(h).start()

        pass_g(h)

    over_heads(own)

    send_far_s.wait_recv()
    send_s.wait_recv()

    def far_step(h):
        send_far_q(h).wait_recv()
        pass_on(q_far, q_next, nq_sem, h)
        dq_add, dk_add, dv_add = pair(
            h,
            1,
            4,
            q_far[h],
            g_far[h],
            stats_far[pl.ds(h, 1), :],
            stats_far[pl.ds(HALF + h, 1), :],
        )
        far_stage[h] = dq_add.astype(BF16)
        back_far(h).start()
        dk_acc[h, 1] += dk_add
        dv_acc[h, 1] += dv_add

    over_heads(far_step)

    first_in = jnp.where(chip % 2 == 1, 1, core)

    def step(h):
        def next_group(n, carry):
            g = lax.rem(first_in + n, 2)
            send_g(h, g).wait_recv()
            send_q(h, g).wait_recv()
            qn, gn = q_next[h, g], g_next[h, g]
            nn, dn = norm_of(stats_next, g, h), delta_of(stats_next, g, h)
            first, dk_add, dv_add = pair(h, 0, 2 + g, qn, gn, nn, dn)
            dk_acc[h, 0] += dk_add
            dv_acc[h, 0] += dv_add
            second, dk_add, dv_add = pair(h, 1, 2 + g, qn, gn, nn, dn)
            dk_acc[h, 1] += dk_add
            dv_acc[h, 1] += dv_add
            next_stage[h, g] = (first + second).astype(BF16)

            back_next(h, g).start()
            return carry

        lax.fori_loop(0, 2, next_group, 0)

        put(
            lambda c: (dk_acc[h, c] * score_scale).astype(BF16), dk_stage, dk_out, ok_sem, h
        )
        put(lambda c: dv_acc[h, c].astype(BF16), dv_stage, dv_out, ov_sem, h)

    over_heads(step)

    def finish(h):
        give_dq(h).wait_recv()
        for half, total in ((core, dq_acc.at[h, core]), (other, dq_given.at[h])):

            @pl.when(core == 0)
            def _():
                back_far_from(h, half).wait_recv()
                total[...] += far_back[h, half].astype(F32)

            back_next_from(h, half).wait_recv()
            grad = total[...] + next_back[h, half].astype(F32)
            dq_out[:, head_cols(half * HALF + h)] = (grad * score_scale).T.astype(BF16)

    over_heads(finish)

    for copy in sq_copies:
        copy.wait_send()
    give_s.wait_send()
    send_s.wait_send()
    send_far_s.wait_send()

    def drain(h):
        give_g(h).wait_send()
        give_v(h).wait_send()
        give_q(h).wait_send()
        give_k(h).wait_send()
        for g in range(2):
            send_g(h, g).wait_send()
            send_q(h, g).wait_send()
            back_next(h, g).wait_send()
        send_far_g(h).wait_send()
        send_far_q(h).wait_send()
        back_far(h).wait_send()
        out_copy(dk_stage, dk_out, ok_sem, h).wait()
        out_copy(dv_stage, dv_out, ov_sem, h).wait()
        give_dq(h).wait_send()

    over_heads(drain)

def store_kernel(*refs):
    ins, outs, sem = refs[:3], refs[3:6], refs[6]
    half = ROWS // 2
    copies = []
    for n in range(3):
        for part in range(2):
            rows = pl.ds(part * half, half)
            copies.append(
                pltpu.make_async_copy(ins[n].at[rows], outs[n].at[rows], sem.at[n, part])
            )
    for copy in copies:
        copy.start()
    for copy in copies:
        copy.wait()

def store(grads, shape):
    return pl.pallas_call(
        store_kernel,
        out_shape=(shape,) * 3,
        in_specs=[pl.BlockSpec(memory_space=pltpu.VMEM)] * 3,
        out_specs=(pl.BlockSpec(memory_space=pl.ANY),) * 3,
        scratch_shapes=[pltpu.SemaphoreType.DMA((3, 2))],
        compiler_params=pltpu.CompilerParams(vmem_limit_bytes=4 * 1024 * 1024),
    )(*grads)

def local(q_raw, k_raw, values, out_grad, attn_out, log_norm, q_gain, k_gain, order):
    seq_count = lax.axis_size("seq")
    head_count = lax.axis_size("head")
    rows, columns = q_raw.shape
    any_spec = pl.BlockSpec(memory_space=pl.ANY)
    vmem_spec = pl.BlockSpec(memory_space=pltpu.VMEM)
    whole = pltpu.VMEM((rows, columns), BF16)
    halves = pltpu.VMEM((HALF, 2, ROWS, HD), BF16)
    single = pltpu.VMEM((HALF, ROWS, HD), BF16)
    flipped = pltpu.VMEM((HALF, 2, HD, ROWS), BF16)
    table = pltpu.VMEM((2, 2 * HALF, ROWS), F32)
    table_one = pltpu.VMEM((2 * HALF, ROWS), F32)
    acc = pltpu.VMEM((HALF, 2, ROWS, HD), F32)
    sem = pltpu.SemaphoreType.DMA
    scratch = [whole] * 4
    scratch += [halves, halves, halves, halves, flipped, table]
    scratch += [single, single, table_one]
    scratch += [pltpu.VMEM((head_count, 2, ROWS), F32)]
    scratch += [halves, halves, table, single, single, table_one]
    scratch += [pltpu.VMEM((HALF, 2, HD, ROWS), F32), acc, acc]
    scratch += [flipped, flipped]
    scratch += [pltpu.VMEM((HALF, HD, ROWS), BF16), flipped]
    scratch += [pltpu.VMEM((HALF, HD, ROWS), F32), single, single]
    scratch += [sem((4,)), sem((HALF,)), sem((HALF,)), sem((2, head_count))]
    scratch += [sem((2, HALF))] * 4 + [sem((2, 1))]
    scratch += [sem((2, HALF, 2))] * 2 + [sem((2, 1))]
    scratch += [sem((2, HALF))] * 2 + [sem((2, 1))]
    scratch += [sem((2, HALF, 2)), sem((2, HALF, 2))]
    scratch += [sem((2, HALF))] * 3
    shape = jax.ShapeDtypeStruct((rows, columns), BF16)
    grads = pl.pallas_call(
        functools.partial(kernel, seq_count, head_count),
        out_shape=(whole,) * 3,
        in_specs=[pl.BlockSpec(memory_space=pltpu.SMEM)] + [any_spec] * 5 + [vmem_spec] * 3,
        out_specs=(vmem_spec,) * 3,
        scratch_shapes=scratch,
        compiler_params=pltpu.CompilerParams(
            collective_id=0, has_side_effects=True, vmem_limit_bytes=62 * 1024 * 1024
        ),
        cost_estimate=pl.CostEstimate(
            flops=10 * 32 * ROWS * ROWS * HD,
            bytes_accessed=8 * rows * columns * 2,
            transcendentals=32 * ROWS * ROWS,
        ),
    )(
        order,
        q_raw,
        k_raw,
        values,
        out_grad,
        attn_out,
        log_norm,
        q_gain.reshape(1, columns),
        k_gain.reshape(1, columns),
    )
    return store(grads, shape)

def solution(mesh):
    placed = P("seq", "head")
    return jax.shard_map(
        local,
        mesh=mesh,
        in_specs=(placed,) * 5 + (P("head", "seq"), P("head"), P("head"), P()),
        out_specs=(placed, placed, placed),
        check_vma=False,
    )
```

```python
import functools

import jax
import jax.numpy as jnp
from jax import lax
from jax.experimental import pallas as pl
from jax.experimental.pallas import tpu as pltpu
from jax.sharding import PartitionSpec as P

EPSILON = 1e-06
LOG2E = 1.4426950408889634
MESH = pl.DeviceIdType.MESH
F32 = jnp.float32
BF16 = jnp.bfloat16
HALF = 4
BLK = 128
ROWS = 256
HD = 128

NT = (((1,), (1,)), ((), ()))
NN = (((1,), (0,)), ((), ()))

def dot(a, b, dims):
    return lax.dot_general(a, b, dims, preferred_element_type=F32)

def head_cols(head):
    return pl.ds(pl.multiple_of(head * HD, HD), HD)

def kernel(
    seq_count,
    head_count,
    order,
    q_hbm,
    k_hbm,
    v_hbm,
    g_hbm,
    o_hbm,
    norm_ref,
    q_gain,
    k_gain,
    dq_out,
    dk_out,
    dv_out,
    q_all,
    k_all,
    g_all,
    o_all,
    q_own,
    g_own,
    k_own,
    v_own,
    k_flip,
    stats,
    q_stage,
    k_stage,
    stats_stage,
    squares,
    q_next,
    g_next,
    stats_next,
    q_far,
    g_far,
    stats_far,
    dq_acc,
    dk_acc,
    dv_acc,
    next_stage,
    next_back,
    far_stage,
    far_back,
    dq_given,
    dk_stage,
    dv_stage,
    load_sem,
    load_g_sem,
    load_v_sem,
    sq_sem,
    xg_sem,
    xv_sem,
    xq_sem,
    xk_sem,
    xs_sem,
    ng_sem,
    nq_sem,
    ns_sem,
    fg_sem,
    fq_sem,
    fs_sem,
    nb_sem,
    fb_sem,
    oq_sem,
    ok_sem,
    ov_sem,
):
    seq = lax.axis_index("seq")
    head = lax.axis_index("head")
    chip = seq // 2
    core = seq % 2
    other = 1 - core
    chips = seq_count // 2
    width = head_count * q_hbm.shape[1]
    score_scale = HD ** (-0.5)

    sibling = (chip * 2 + other, head)
    prev = (((chip + chips - 1) % chips) * 2 + core, head)
    succ = (((chip + 1) % chips) * 2 + core, head)
    prev_far = (((chip + chips - 2) % chips) * 2 + core, head)
    succ_far = (((chip + 2) % chips) * 2 + core, head)

    def on_core(device, which):
        return (device[0] // 2 * 2 + which, head)

    def remote(src, dst, sem, idx, device, there=None):
        return pltpu.make_async_remote_copy(
            src_ref=src,
            dst_ref=dst,
            send_sem=sem.at[(0, *idx)],
            recv_sem=sem.at[(1, *(there or idx))],
            device_id=device,
            device_id_type=MESH,
        )

    barrier = pltpu.get_barrier_semaphore()

    def signal(sem, device):
        pl.semaphore_signal(sem, inc=1, device_id=device, device_id_type=MESH)

    for device in (sibling, succ, succ_far, on_core(prev, 0), on_core(prev, 1)):
        signal(barrier, device)

    @pl.when(core == 0)
    def _():
        signal(barrier, on_core(prev_far, 0))
        signal(barrier, on_core(prev_far, 1))

    for n in range(1, head_count):
        signal(barrier, (seq, (head + n) % head_count))

    loads = [
        pltpu.make_async_copy(src, dst, load_sem.at[n])
        for n, (src, dst) in enumerate(
            ((q_hbm, q_all), (k_hbm, k_all), (g_hbm, g_all), (o_hbm, o_all))
        )
    ]

    def load_g(h):
        return pltpu.make_async_copy(
            g_hbm.at[:, head_cols(core * HALF + h)], g_own.at[h, core], load_g_sem.at[h]
        )

    def load_v(h):
        return pltpu.make_async_copy(
            v_hbm.at[:, head_cols(core * HALF + h)], v_own.at[h, core], load_v_sem.at[h]
        )

    for h in range(HALF):
        load_g(h).start()
    loads[0].start()
    loads[1].start()
    loads[2].start()
    loads[3].start()
    for h in range(HALF):
        load_v(h).start()

    def row_sums(src):
        def add(h, total):
            block = src[:, head_cols(h)].astype(F32)
            return total + block * block

        total = lax.fori_loop(0, 2 * HALF, add, jnp.zeros((ROWS, HD), F32))
        return jnp.sum(total.T, axis=0, keepdims=True)

    def sum_squares():
        loads[0].wait()
        loads[1].wait()
        squares[0, 0:1, :] = row_sums(q_all)
        squares[0, 1:2, :] = row_sums(k_all)

    def make_stats():
        loads[2].wait()
        loads[3].wait()
        norm_rows = norm_ref[...] * LOG2E

        def delta_row(h):
            product = g_all[:, head_cols(h)].astype(F32) * o_all[:, head_cols(h)].astype(F32)
            return jnp.sum(product.T, axis=0, keepdims=True)

        first_half = core == 0
        stats[core, 0:HALF, :] = jnp.where(first_half, norm_rows[0:HALF], norm_rows[HALF:])
        stats_stage[0:HALF, :] = jnp.where(first_half, norm_rows[HALF:], norm_rows[0:HALF])
        for h in range(HALF):
            stats[core, HALF + h : HALF + h + 1, :] = delta_row(core * HALF + h)
            stats_stage[HALF + h : HALF + h + 1, :] = delta_row(other * HALF + h)

    sum_squares()
    make_stats()

    pl.semaphore_wait(barrier, 6 + head_count - 1)

    def give_g(h):
        return remote(
            g_hbm.at[:, head_cols(other * HALF + h)], g_own.at[h, core], xg_sem, (h,), sibling
        )

    def give_v(h):
        return remote(
            v_hbm.at[:, head_cols(other * HALF + h)], v_own.at[h, core], xv_sem, (h,), sibling
        )

    def give_q(h):
        return remote(q_stage.at[h], q_own.at[h, core], xq_sem, (h,), sibling)

    def give_k(h):
        return remote(k_stage.at[h], k_own.at[h, core], xk_sem, (h,), sibling)

    give_s = remote(stats_stage, stats.at[core], xs_sem, (0,), sibling)

    def send_g(h, g):
        return remote(g_own.at[h, g], g_next.at[h, g], ng_sem, (h, g), prev)

    def send_q(h, g):
        return remote(q_own.at[h, g], q_next.at[h, g], nq_sem, (h, g), prev)

    send_s = remote(stats, stats_next, ns_sem, (0,), prev)

    def send_far_g(h):
        return remote(g_own.at[h, 0], g_far.at[h], fg_sem, (h,), prev_far)

    def send_far_q(h):
        return remote(q_own.at[h, 0], q_far.at[h], fq_sem, (h,), prev_far)

    send_far_s = remote(stats.at[0], stats_far, fs_sem, (0,), prev_far)

    def back_next(h, g):
        return remote(
            next_stage.at[h, g], next_back.at[h, core], nb_sem, (h, g), on_core(succ, g), (h, core)
        )

    def back_far(h):
        return remote(
            far_stage.at[h], far_back.at[h, core], fb_sem, (h, 0), on_core(succ_far, 0), (h, core)
        )

    def back_next_from(h, half):
        return remote(
            next_stage.at[h, 0], next_back.at[h, half], nb_sem, (h, 0), sibling, (h, half)
        )

    def back_far_from(h, half):
        return remote(far_stage.at[h], far_back.at[h, half], fb_sem, (h, 0), sibling, (h, half))

    def give_dq(h):
        return remote(dq_acc.at[h, other], dq_given.at[h], oq_sem, (h,), sibling)

    def over_heads(body, first=0, last=HALF):
        lax.fori_loop(first, last, lambda h, c: (body(h), c)[1], 0)

    def start_next(send, h, g):
        @pl.when(g + chip % 2 > 0)
        def _():
            send(h, g).start()

    def start_far(send, h, g):
        @pl.when(g == 0)
        def _():
            send(h).start()

    def pass_on(src, dst, sem, h):
        @pl.when(chip % 2 == 0)
        def _():
            remote(src.at[h], dst.at[h, 0], sem, (h, 0), succ).start()

    def first_g(h):
        load_g(h).wait()
        start_next(send_g, h, core)

    sq_copies = []
    for n in range(1, head_count):
        copy = remote(
            squares.at[0], squares.at[n], sq_sem, (n,), (seq, (head + n) % head_count)
        )
        copy.start()
        sq_copies.append(copy)

    give_s.start()
    over_heads(lambda h: give_g(h).start())
    over_heads(first_g)
    over_heads(lambda h: give_v(h).start())

    def second_g(h):
        give_g(h).wait_recv()
        start_next(send_g, h, other)

    over_heads(second_g)
    over_heads(lambda h: send_far_g(h).start())

    for copy in sq_copies:
        copy.wait_recv()
    give_s.wait_recv()
    send_s.start()
    send_far_s.start()
    total = squares[0]
    for n in range(1, head_count):
        total = total + squares[n]
    scale = lax.rsqrt(total / width + EPSILON)
    q_scale = jnp.broadcast_to(scale[0:1, :], (HD, ROWS)).T
    k_scale = jnp.broadcast_to(scale[1:2, :], (HD, ROWS)).T

    def normed(src, scales, gain, h):
        return (src[:, head_cols(h)].astype(F32) * scales * gain[0:1, head_cols(h)]).astype(BF16)

    def norm_q(h):
        q_stage[h] = normed(q_all, q_scale, q_gain, other * HALF + h)
        give_q(h).start()
        q_own[h, core] = normed(q_all, q_scale, q_gain, core * HALF + h)

    over_heads(norm_q)

    def queue_far_q(h):
        @pl.when(core == 1)
        def _():
            give_q(h).wait_recv()

        send_far_q(h).start()

    def queue_q(h):
        start_next(send_q, h, core)

        @pl.when(core == 0)
        def _():
            give_q(h).wait_recv()

        start_next(send_q, h, other)

    def queue_odd_q(h):
        send_q(h, core).start()
        give_q(h).wait_recv()
        send_q(h, other).start()
        send_far_q(h).start()

    @pl.when(chip % 2 == 0)
    def _():
        over_heads(queue_far_q)
        over_heads(queue_q)

    @pl.when(chip % 2 == 1)
    def _():
        over_heads(queue_odd_q)

    def pass_g(h):
        send_far_g(h).wait_recv()
        pass_on(g_far, g_next, ng_sem, h)

    def norm_k(h):
        k_stage[h] = normed(k_all, k_scale, k_gain, other * HALF + h)
        give_k(h).start()
        mine = normed(k_all, k_scale, k_gain, core * HALF + h)
        k_own[h, core] = mine
        k_flip[h, core] = mine.T

    over_heads(norm_k)

    def ready_kv(h):
        give_k(h).wait_recv()
        k_flip[h, other] = k_own[h, other].T
        give_v(h).wait_recv()
        load_v(h).wait()

    over_heads(ready_kv)

    def group_of(step):
        return (chip * 2 + step) % seq_count

    def blocks_of(step):
        group = group_of(step)
        return order[2 * group], order[2 * group + 1]

    def pair(h, c, step, q, g, norm_row, delta):
        s = dot(k_own[h, c], q, NT)
        d = dot(v_own[h, c], g, NT)
        query_at, key_at = blocks_of(step), blocks_of(c)
        col = lax.broadcasted_iota(jnp.int32, (1, ROWS), 1)
        parts = []
        for half in range(2):
            scaled = s[half * BLK : (half + 1) * BLK] * (score_scale * LOG2E)
            if isinstance(step, int) and step == c:
                query_pos = jnp.where(
                    col < BLK, query_at[0] * BLK, query_at[1] * BLK - BLK
                ) + col
                key_pos = key_at[half] * BLK + lax.broadcasted_iota(jnp.int32, (BLK, ROWS), 0)
                part = jnp.where(key_pos <= query_pos, jnp.exp2(scaled - norm_row), 0.0)
            else:
                hidden = [jnp.where(key_at[half] > at, 1e30, 0.0) for at in query_at]
                part = jnp.exp2(scaled - (norm_row + jnp.where(col < BLK, hidden[0], hidden[1])))
            parts.append(part)
        p = jnp.concatenate(parts, axis=0)
        ds = (p * (d - delta)).astype(BF16)
        dv_add = dot(p.astype(BF16), g, NN)
        dk_add = dot(ds, q, NN)
        dq_add = dot(k_flip[h, c], ds, NN)
        return dq_add, dk_add, dv_add

    def out_copy(stage, out, sem, h):
        return remote(
            stage.at[h], out.at[:, head_cols(core * HALF + h)], sem, (h,), sibling
        )

    def put(value_of, stage, out, sem, h):
        stage[h] = value_of(other)
        out_copy(stage, out, sem, h).start()
        out[:, head_cols(core * HALF + h)] = value_of(core)

    norm_of = lambda ref, g, h: ref[g, pl.ds(h, 1), :]
    delta_of = lambda ref, g, h: ref[g, pl.ds(HALF + h, 1), :]

    def own(h):
        q0, g0, q1, g1 = q_own[h, 0], g_own[h, 0], q_own[h, 1], g_own[h, 1]
        n0, d0 = norm_of(stats, 0, h), delta_of(stats, 0, h)
        n1, d1 = norm_of(stats, 1, h), delta_of(stats, 1, h)
        dq_add, dk_add, dv_add = pair(h, 0, 0, q0, g0, n0, d0)
        dq_acc[h, 0] = dq_add
        dk_acc[h, 0] = dk_add
        dv_acc[h, 0] = dv_add
        dq_add, dk_add, dv_add = pair(h, 0, 1, q1, g1, n1, d1)
        dq_acc[h, 1] = dq_add
        dk_acc[h, 0] += dk_add
        dv_acc[h, 0] += dv_add
        dq_add, dk_add, dv_add = pair(h, 1, 1, q1, g1, n1, d1)
        dq_acc[h, 1] += dq_add
        dk_acc[h, 1] = dk_add
        dv_acc[h, 1] = dv_add
        give_dq(h).start()

        pass_g(h)

    over_heads(own)

    send_far_s.wait_recv()
    send_s.wait_recv()

    def far_step(h):
        send_far_q(h).wait_recv()
        pass_on(q_far, q_next, nq_sem, h)
        dq_add, dk_add, dv_add = pair(
            h,
            1,
            4,
            q_far[h],
            g_far[h],
            stats_far[pl.ds(h, 1), :],
            stats_far[pl.ds(HALF + h, 1), :],
        )
        far_stage[h] = dq_add.astype(BF16)
        back_far(h).start()
        dk_acc[h, 1] += dk_add
        dv_acc[h, 1] += dv_add

    over_heads(far_step)

    first_in = jnp.where(chip % 2 == 1, 1, core)

    def step(h):
        def next_group(n, carry):
            g = lax.rem(first_in + n, 2)
            send_g(h, g).wait_recv()
            send_q(h, g).wait_recv()
            qn, gn = q_next[h, g], g_next[h, g]
            nn, dn = norm_of(stats_next, g, h), delta_of(stats_next, g, h)
            first, dk_add, dv_add = pair(h, 0, 2 + g, qn, gn, nn, dn)
            dk_acc[h, 0] += dk_add
            dv_acc[h, 0] += dv_add
            second, dk_add, dv_add = pair(h, 1, 2 + g, qn, gn, nn, dn)
            dk_acc[h, 1] += dk_add
            dv_acc[h, 1] += dv_add
            next_stage[h, g] = (first + second).astype(BF16)

            back_next(h, g).start()
            return carry

        lax.fori_loop(0, 2, next_group, 0)

        put(
            lambda c: (dk_acc[h, c] * score_scale).astype(BF16), dk_stage, dk_out, ok_sem, h
        )
        put(lambda c: dv_acc[h, c].astype(BF16), dv_stage, dv_out, ov_sem, h)

    over_heads(step)

    def finish(h):
        give_dq(h).wait_recv()
        for half, total in ((core, dq_acc.at[h, core]), (other, dq_given.at[h])):

            @pl.when(core == 0)
            def _():
                back_far_from(h, half).wait_recv()
                total[...] += far_back[h, half].astype(F32)

            back_next_from(h, half).wait_recv()
            grad = total[...] + next_back[h, half].astype(F32)
            dq_out[:, head_cols(half * HALF + h)] = (grad * score_scale).T.astype(BF16)

    over_heads(finish)

    for copy in sq_copies:
        copy.wait_send()
    give_s.wait_send()
    send_s.wait_send()
    send_far_s.wait_send()

    def drain(h):
        give_g(h).wait_send()
        give_v(h).wait_send()
        give_q(h).wait_send()
        give_k(h).wait_send()
        for g in range(2):
            send_g(h, g).wait_send()
            send_q(h, g).wait_send()
            back_next(h, g).wait_send()
        send_far_g(h).wait_send()
        send_far_q(h).wait_send()
        back_far(h).wait_send()
        out_copy(dk_stage, dk_out, ok_sem, h).wait()
        out_copy(dv_stage, dv_out, ov_sem, h).wait()
        give_dq(h).wait_send()

    over_heads(drain)

def store_kernel(*refs):
    ins, outs, sem = refs[:3], refs[3:6], refs[6]
    half = ROWS // 2
    copies = []
    for n in range(3):
        for part in range(2):
            rows = pl.ds(part * half, half)
            copies.append(
                pltpu.make_async_copy(ins[n].at[rows], outs[n].at[rows], sem.at[n, part])
            )
    for copy in copies:
        copy.start()
    for copy in copies:
        copy.wait()

def store(grads, shape):
    return pl.pallas_call(
        store_kernel,
        out_shape=(shape,) * 3,
        in_specs=[pl.BlockSpec(memory_space=pltpu.VMEM)] * 3,
        out_specs=(pl.BlockSpec(memory_space=pl.ANY),) * 3,
        scratch_shapes=[pltpu.SemaphoreType.DMA((3, 2))],
        compiler_params=pltpu.CompilerParams(vmem_limit_bytes=4 * 1024 * 1024),
    )(*grads)

def local(q_raw, k_raw, values, out_grad, attn_out, log_norm, q_gain, k_gain, order):
    seq_count = lax.axis_size("seq")
    head_count = lax.axis_size("head")
    rows, columns = q_raw.shape
    any_spec = pl.BlockSpec(memory_space=pl.ANY)
    vmem_spec = pl.BlockSpec(memory_space=pltpu.VMEM)
    whole = pltpu.VMEM((rows, columns), BF16)
    halves = pltpu.VMEM((HALF, 2, ROWS, HD), BF16)
    single = pltpu.VMEM((HALF, ROWS, HD), BF16)
    flipped = pltpu.VMEM((HALF, 2, HD, ROWS), BF16)
    table = pltpu.VMEM((2, 2 * HALF, ROWS), F32)
    table_one = pltpu.VMEM((2 * HALF, ROWS), F32)
    acc = pltpu.VMEM((HALF, 2, ROWS, HD), F32)
    sem = pltpu.SemaphoreType.DMA
    scratch = [whole] * 4
    scratch += [halves, halves, halves, halves, flipped, table]
    scratch += [single, single, table_one]
    scratch += [pltpu.VMEM((head_count, 2, ROWS), F32)]
    scratch += [halves, halves, table, single, single, table_one]
    scratch += [pltpu.VMEM((HALF, 2, HD, ROWS), F32), acc, acc]
    scratch += [flipped, flipped]
    scratch += [pltpu.VMEM((HALF, HD, ROWS), BF16), flipped]
    scratch += [pltpu.VMEM((HALF, HD, ROWS), F32), single, single]
    scratch += [sem((4,)), sem((HALF,)), sem((HALF,)), sem((2, head_count))]
    scratch += [sem((2, HALF))] * 4 + [sem((2, 1))]
    scratch += [sem((2, HALF, 2))] * 2 + [sem((2, 1))]
    scratch += [sem((2, HALF))] * 2 + [sem((2, 1))]
    scratch += [sem((2, HALF, 2)), sem((2, HALF, 2))]
    scratch += [sem((2, HALF))] * 3
    shape = jax.ShapeDtypeStruct((rows, columns), BF16)
    grads = pl.pallas_call(
        functools.partial(kernel, seq_count, head_count),
        out_shape=(whole,) * 3,
        in_specs=[pl.BlockSpec(memory_space=pltpu.SMEM)] + [any_spec] * 5 + [vmem_spec] * 3,
        out_specs=(vmem_spec,) * 3,
        scratch_shapes=scratch,
        compiler_params=pltpu.CompilerParams(
            collective_id=0, has_side_effects=True, vmem_limit_bytes=62 * 1024 * 1024
        ),
        cost_estimate=pl.CostEstimate(
            flops=10 * 32 * ROWS * ROWS * HD,
            bytes_accessed=8 * rows * columns * 2,
            transcendentals=32 * ROWS * ROWS,
        ),
    )(
        order,
        q_raw,
        k_raw,
        values,
        out_grad,
        attn_out,
        log_norm,
        q_gain.reshape(1, columns),
        k_gain.reshape(1, columns),
    )
    return store(grads, shape)

def solution(mesh):
    placed = P("seq", "head")
    return jax.shard_map(
        local,
        mesh=mesh,
        in_specs=(placed,) * 5 + (P("head", "seq"), P("head"), P("head"), P()),
        out_specs=(placed, placed, placed),
        check_vma=False,
    )
```
